32 devices in a mesh: kgrp: 2 (over y), orb: 16 (over z, x, core).
Axes of the slice: x: 2, y: 2, z: 4, core: 2. Of those that a mesh axis runs over, the one named last changes fastest.
Arguments:
- hopping_tiles: bfloat16 [32, 12, 96, 128], P('orb'), may hold values from -0.109375 to 0.109375
- tile_strip: int32 [32, 12, 1], replicated, may hold values from 0 to 15; in each aligned block of 24 rows (0 to 23, 24 to 47, ..., all dimensions but the last counted through in order) at most 2 rows name the same one
- tile_column_slot: int32 [32, 12], replicated, may hold values from 0 to 1
- lattice: int32 [32, 3], replicated, may hold values from -6 to 6
- kpoints: float32 [4, 3], P('kgrp'), parts along dimension 0, may hold values from 0 to 1
- start_block: bfloat16 [1536, 8192], P('orb'), may hold values from -6 to 6
Outputs:
- filtered: bfloat16 [4, 2, 1536, 8192], P('kgrp', None, 'orb'), parts along dimension 0
The draws below stay inside these ranges and needn't reach their ends.
There are 2 independent parts, one for each index of `kgrp`. The reference program is written for one: setup_inputs(seed, part) draws one part's arguments, and reference() takes and returns one part's arrays. A program takes and returns all parts, laid end to end along the dimension named above; an argument that names none is the same for every part. Nothing has to cross between parts.
Inputs may be any that keep to these rules, and one draw needn't show every extreme that they name: `tile_strip`: among the 24 tiles of the lattice vectors r with the same r // 2 (one owner), no strip is named more than 2 times, and in every draw some strip is named exactly 2 times.
All inputs are finite; a program needn't handle non-finite values.
Results may differ from the reference program's by a relative error of at most 0.0065.
Values may be sent and summed in bfloat16 or wider, within the bound.
No kernel may reach another device: no remote copies, remote signals or barrier semaphores. Data moves between devices by JAX's collectives and lax.ppermute only.
A program may use at most 128 MiB of HBM per device.

```python
import math
import jax
import jax.numpy as jnp
import numpy as np
from jax import lax

STRIP_ROWS = 96
TILE_WIDTH = 128
HALO = 80
STEPS = 2
CAP = 2
KPOINT_COUNT = 2
NV = 8192
NORB = 1536
LATTICE_COUNT = 32
NONZERO_TILES = 12
BANDW = 256
SLOT_TOTAL = 2
N_ORB = 16


def with_ends(result, stream_key, low, largest):
    dims = result.shape
    place = [jax.random.randint(jax.random.fold_in(stream_key, axis), (), 0, dims[axis]) for axis in range(len(dims))]
    result = result.at[tuple(place)].set(low)
    longest = dims.index(max(dims))
    place[longest] = (place[longest] + 1) % dims[longest]
    return result.at[tuple(place)].set(largest)


def block_levels(rng, shape, split, low, high):
    gain, own = 1.0, jax.random.fold_in(rng, 6)
    for position, parts in split:
        steps = jnp.exp(jax.random.uniform(jax.random.fold_in(own, position), (parts,), jnp.float32, low / len(split), high / len(split)))
        gain = gain * jnp.repeat(steps, shape[position] // parts).reshape([-1 if axis == position else 1 for axis in range(len(shape))])
    return gain


def assign_block(key, own, number, rows, number_of, top, reach, skew):
    sequence = jax.random.permutation(key, number_of)
    heavy_load, ordinary = portions_of(number_of, rows * top, reach, skew, True), portions_of(number_of, rows * top, reach, skew, False)
    places = jnp.arange(number_of)

    def named(lengths, rotation):
        used = int((lengths > 0).sum())
        fixed = max(1, used // 4)
        passed = fixed + (places - fixed + rotation * (used - fixed)) % max(1, number_of - fixed)
        return jnp.zeros((number_of,), jnp.int32).at[sequence[jnp.where(places < fixed, places, passed)]].set(jnp.asarray(lengths, jnp.int32))

    lengths = jnp.where(number % 4 == 0, named(heavy_load, number // 4), named(ordinary, number - number // 4 - 1))
    mixed = jax.random.permutation(jax.random.fold_in(own, 3), number_of)
    source_of, receiver = mixed[0:number_of // 2 * 2:2], mixed[1:number_of // 2 * 2:2]
    margin = jnp.minimum(lengths[source_of] - 1, reach - lengths[receiver]) // 2
    margin = jnp.where((source_of == sequence[0]) | (receiver == sequence[0]) | (lengths[receiver] == 0), 0, jnp.maximum(margin, 0))
    passed = jax.random.randint(jax.random.fold_in(own, 4), (number_of // 2,), 0, 1 << 20) % (margin + 1)
    lengths = lengths.at[source_of].add(-passed).at[receiver].add(passed)
    members = jnp.searchsorted(jnp.cumsum(lengths), jnp.arange(rows * top), side="right").astype(jnp.int32)
    listing = members.reshape(top, rows).T
    listing = listing[jax.random.permutation(jax.random.fold_in(own, 1), rows)]
    rotation = jax.random.randint(jax.random.fold_in(own, 2), (rows, 1), 0, top)
    return jnp.take_along_axis(listing, (jnp.arange(top)[None, :] + rotation) % top, axis=1)


def portions_of(amount, total, bound, lean, full):
    weights = [(1 << 20) // math.isqrt(rank ** lean) + 1 for rank in range(1, amount + 1)]
    largest = bound if full else min(bound, max(-(-total // amount), total * weights[0] // sum(weights)))
    least = 1 if total - largest >= amount - 1 else 0
    given, surplus = [largest] + [least] * (amount - 1), total - largest - least * (amount - 1)
    while surplus > 0:
        candidates = [i for i in range(1, amount) if given[i] < largest] or [i for i in range(1, amount) if given[i] < bound]
        mass, remaining = sum([weights[i] for i in candidates]), surplus
        for i in candidates:
            extra = min(bound - given[i], max(1, remaining * weights[i] // mass), surplus)
            given[i] = given[i] + extra
            surplus = surplus - extra
    return np.array(given)


def bell_draw(rng, extent, deviation, limit, cuts=(), kind=jnp.bfloat16):
    array = jax.random.normal(rng, extent, jnp.float32) * deviation
    if len(cuts) > 0:
        array = block_levels(rng, extent, cuts, -0.22, 0.18) * array
    return jnp.clip(array, min=-limit, max=limit).astype(kind)


def setup_inputs(seed: int = 0, part: int = 0) -> dict:
    arg_keys = jax.random.split(jax.random.key(seed), 7)
    part_keys = jax.random.split(jax.random.fold_in(arg_keys[6], part), 7)
    hopping_tiles = bell_draw(arg_keys[0], (LATTICE_COUNT, NONZERO_TILES, STRIP_ROWS, TILE_WIDTH), (TILE_WIDTH * STEPS * NONZERO_TILES) ** -0.5, 0.109375, ((0, 16),))
    tile_strip_keys = jax.random.split(jax.random.fold_in(arg_keys[1], 1), LATTICE_COUNT * NONZERO_TILES // (STEPS * NONZERO_TILES))
    tile_strip_turns = jax.random.permutation(jax.random.fold_in(arg_keys[1], 3), LATTICE_COUNT * NONZERO_TILES // (STEPS * NONZERO_TILES))
    tile_strip = jax.vmap(lambda own, number: assign_block(jax.random.fold_in(arg_keys[1], 2), own, number, STEPS * NONZERO_TILES, N_ORB, 1, CAP, 2))(tile_strip_keys, tile_strip_turns).reshape((LATTICE_COUNT, NONZERO_TILES, 1))
    tile_column_slot = with_ends(jax.random.randint(arg_keys[2], (LATTICE_COUNT, NONZERO_TILES), 0, SLOT_TOTAL), jax.random.fold_in(arg_keys[2], 1), 0, SLOT_TOTAL - 1).astype(jnp.int32)
    lattice = with_ends(jax.random.randint(arg_keys[3], (LATTICE_COUNT, 3), -6, 7), jax.random.fold_in(arg_keys[3], 1), -6, 6).astype(jnp.int32)
    kpoints = jnp.clip(jax.random.uniform(part_keys[4], (KPOINT_COUNT, 3), jnp.float32, 0.0, 1.0), 0.0, 1.0)
    start_block = bell_draw(arg_keys[5], (NORB, NV), 1.0, 6.0, ((0, 16),))
    return dict(hopping_tiles=hopping_tiles, tile_strip=tile_strip, tile_column_slot=tile_column_slot, lattice=lattice, kpoints=kpoints, start_block=start_block)


def phase_table(lattice, kpoints):
    cell_float = lattice.astype(jnp.float32)
    fraction = (kpoints[None, :, 0] * cell_float[:, None, 0] + kpoints[None, :, 1] * cell_float[:, None, 1]) + kpoints[None, :, 2] * cell_float[:, None, 2]
    radians = 6.283185307179586 * fraction
    return jnp.stack([jnp.cos(radians), jnp.sin(radians)], axis=-1).astype(jnp.bfloat16)


def reference(hopping_tiles, tile_strip, tile_column_slot, lattice, kpoints, start_block):
    phases = lax.optimization_barrier(phase_table(lattice, kpoints)).astype(jnp.float32)
    strips = tile_strip[:, :, 0]

    def add_vector(running_total, scan_item):
        tile_block, strip_row, slot_row, phase_row = scan_item
        contribution = phase_row[None, :, :, None, None] * tile_block.astype(jnp.float32)[:, None, None, :, :]
        return running_total.at[strip_row, slot_row].add(contribution), None

    running_total = jnp.zeros((N_ORB, SLOT_TOTAL, KPOINT_COUNT, 2, STRIP_ROWS, TILE_WIDTH), jnp.float32)
    running_total, _ = lax.scan(add_vector, running_total, (hopping_tiles, strips, tile_column_slot, phases))
    banded_hamiltonian = running_total.transpose(0, 2, 3, 4, 1, 5).reshape(N_ORB, KPOINT_COUNT, 2, STRIP_ROWS, SLOT_TOTAL * TILE_WIDTH).astype(jnp.bfloat16)
    strip_ids = jnp.arange(N_ORB, dtype=jnp.int32)

    padded_start = jnp.pad(start_block, ((HALO, HALO), (0, 0)))

    def first_strip(strip_index):
        window = lax.dynamic_slice_in_dim(padded_start, strip_index * STRIP_ROWS, BANDW, 0).astype(jnp.float32)
        return jnp.einsum('kprb,bv->kprv', banded_hamiltonian[strip_index].astype(jnp.float32), window).astype(jnp.bfloat16)

    first_pass = lax.map(first_strip, strip_ids)
    first_pass = first_pass.transpose(1, 2, 0, 3, 4).reshape(KPOINT_COUNT, 2, NORB, NV)
    padded_first = jnp.pad(first_pass, ((0, 0), (0, 0), (HALO, HALO), (0, 0)))

    def second_strip(strip_index):
        window = lax.dynamic_slice_in_dim(padded_first, strip_index * STRIP_ROWS, BANDW, 2).astype(jnp.float32)
        product = jnp.einsum('kprb,kqbv->kpqrv', banded_hamiltonian[strip_index].astype(jnp.float32), window)
        own_rows = lax.dynamic_slice_in_dim(start_block, strip_index * STRIP_ROWS, STRIP_ROWS, 0).astype(jnp.float32)
        real_part = 2.0 * (product[:, 0, 0] - product[:, 1, 1]) - own_rows[None]
        imag_part = 2.0 * (product[:, 0, 1] + product[:, 1, 0])
        return jnp.stack([real_part, imag_part], axis=1).astype(jnp.bfloat16)

    second_pass = lax.map(second_strip, strip_ids)
    return second_pass.transpose(1, 2, 0, 3, 4).reshape(KPOINT_COUNT, 2, NORB, NV)
```

```python
import functools

import jax
import jax.numpy as jnp
from jax import lax
from jax.experimental import pallas as pl
from jax.experimental.pallas import tpu as pltpu
from jax.sharding import PartitionSpec as P

HALO = 80
CAP = 2
PIECES = 2
BLOCK = 1024


def routed(value, route):
    groups, owners = lax.axis_size("kgrp"), lax.axis_size("orb")
    pairs = []
    for group in range(groups):
        for owner in range(owners):
            to_group, to_owner = route(group, owner)
            if 0 <= to_owner < owners:
                pairs.append((group * owners + owner, to_group * owners + to_owner))
    return lax.ppermute(value, ("kgrp", "orb"), pairs)


def to_sibling(value):
    return routed(value, lambda group, owner: (group, owner ^ 1))


def to_pair_chip(value):
    return routed(value, lambda group, owner: (group, owner ^ 2))


def onward(value):
    return routed(value, lambda group, owner: (group, owner + (4 if owner & 2 == 0 else -4)))


def to_other_group(value):
    return routed(value, lambda group, owner: (1 - group, owner))


def shifted(value, steps):
    return routed(value, lambda group, owner: (group, owner + steps))


def phase_table(lattice, kpoints):
    cell_float = lattice.astype(jnp.float32)
    fraction = (
        kpoints[None, :, 0] * cell_float[:, None, 0]
        + kpoints[None, :, 1] * cell_float[:, None, 1]
        + kpoints[None, :, 2] * cell_float[:, None, 2]
    )
    radians = 6.283185307179586 * fraction
    return jnp.stack([jnp.cos(radians), jnp.sin(radians)], axis=-1).astype(jnp.bfloat16)


def pack_kernel(tile_count, dest_ref, tiles_ref, packed_ref, source, placed, sems):
    slots = packed_ref.shape[0]

    def clear(slot, carry):
        source[slot] = 0
        return carry

    def forget(owner, carry):
        placed[owner] = 0
        return carry

    def place(tile, carry):
        dest = dest_ref[tile]
        rank = placed[dest]
        placed[dest] = rank + 1
        source[dest * CAP + rank] = tile
        return carry

    lax.fori_loop(0, slots, clear, 0)
    lax.fori_loop(0, slots // CAP, forget, 0)
    lax.fori_loop(0, tile_count, place, 0)

    def copy(slot):
        return pltpu.make_async_copy(tiles_ref.at[source[slot]], packed_ref.at[slot], sems.at[slot])

    def start(slot, carry):
        copy(slot).start()
        return carry

    def wait(slot, carry):
        copy(slot).wait()
        return carry

    lax.fori_loop(0, slots, start, 0)
    lax.fori_loop(0, slots, wait, 0)


def pack_tiles(tiles, own_dest, owners):
    tile_count = tiles.shape[0]
    slots = owners * CAP
    return pl.pallas_call(
        functools.partial(pack_kernel, tile_count),
        out_shape=jax.ShapeDtypeStruct((slots,) + tiles.shape[1:], tiles.dtype),
        grid_spec=pltpu.PrefetchScalarGridSpec(
            num_scalar_prefetch=1,
            grid=(1,),
            in_specs=[pl.BlockSpec(memory_space=pl.ANY)],
            out_specs=pl.BlockSpec(memory_space=pl.ANY),
            scratch_shapes=[
                pltpu.SMEM((slots,), jnp.int32),
                pltpu.SMEM((owners,), jnp.int32),
                pltpu.SemaphoreType.DMA((slots,)),
            ],
        ),
        name="pack_tiles",
    )(own_dest, tiles)


def receive_weights(dest_all, slot_all, phases, device, slot_count):
    owners, step_count, tile_count = dest_all.shape
    k_count = phases.shape[1]
    total = step_count * tile_count
    mine = dest_all.reshape(owners, total) == device
    before = jnp.tril(jnp.ones((total, total), jnp.int32), -1)
    rank = jnp.sum(mine.astype(jnp.int32)[:, None, :] * before[None], axis=-1)
    column = slot_all.reshape(owners, total)
    phase_all = jnp.broadcast_to(
        phases.reshape(owners, step_count, 1, k_count * 2), (owners, step_count, tile_count, k_count * 2)
    ).reshape(owners, total, k_count * 2)
    chosen = (
        mine[None, None, :, :]
        & (rank[None, None] == jnp.arange(CAP, dtype=jnp.int32)[:, None, None, None])
        & (column[None, None] == jnp.arange(slot_count, dtype=jnp.int32)[None, :, None, None])
    )
    weights = jnp.sum(
        jnp.where(chosen[None], phase_all.transpose(2, 0, 1)[:, None, None], 0.0), axis=-1
    )
    return weights.transpose(0, 2, 3, 1).reshape(k_count * 2 * slot_count, owners * CAP)


def band_kernel(k_count, slot_count, weight_ref, tiles_ref, pair_ref, tail_ref, head_ref):
    slots, rows, width = tiles_ref.shape
    part = rows // 2
    band = slot_count * width
    kinds = k_count * 2 * slot_count
    for low in (0, part):

        def add(slot, totals):
            tile = tiles_ref[slot, low : low + part, :].astype(jnp.float32)
            return tuple(total + weight_ref[kind, slot] * tile for kind, total in enumerate(totals))

        totals = lax.fori_loop(
            0, slots, add, tuple(jnp.zeros((part, width), jnp.float32) for _ in range(kinds)), unroll=2
        )
        for k in range(k_count):
            for p in range(2):
                for j in range(slot_count):
                    value = totals[(k * 2 + p) * slot_count + j].astype(jnp.bfloat16)
                    columns = slice(j * width, (j + 1) * width)
                    later = slice(band + j * width, band + (j + 1) * width)
                    if p == 0:
                        pair_ref[k, low : low + part, columns] = value
                        pair_ref[k, rows + low : rows + low + part, later] = value
                    else:
                        pair_ref[k, rows + low : rows + low + part, columns] = value
                        pair_ref[k, low : low + part, later] = -value
    for k in range(k_count):
        for p in range(2):
            tail_ref[k, p] = pair_ref[k, (p + 1) * rows - HALO : (p + 1) * rows, 0:band]
            head_ref[k, p] = pair_ref[k, p * rows : p * rows + HALO, 0:band]


def make_bands(weights, tiles, k_count, slot_count):
    rows, width = tiles.shape[1:]
    band = slot_count * width
    vmem = pl.BlockSpec(memory_space=pltpu.VMEM)
    edge = jax.ShapeDtypeStruct((k_count, 2, HALO, band), jnp.bfloat16)
    return pl.pallas_call(
        functools.partial(band_kernel, k_count, slot_count),
        out_shape=[jax.ShapeDtypeStruct((k_count, 2 * rows, 2 * band), jnp.bfloat16), edge, edge],
        in_specs=[pl.BlockSpec(memory_space=pltpu.SMEM), vmem],
        out_specs=[vmem, vmem, vmem],
        compiler_params=pltpu.CompilerParams(vmem_limit_bytes=40 * 1024 * 1024),
        name="make_bands",
    )(weights, tiles)


def filter_kernel(
    steps,
    where_ref,
    pair_ref,
    left_ref,
    right_ref,
    own_ref,
    sibling_ref,
    near_ref,
    chip_ref,
    onward_ref,
    *rest,
):
    out_ref, window, sems = rest[-3:]
    k_count, double_rows, _ = pair_ref.shape
    rows = double_rows // 2
    band = left_ref.shape[-1]
    block = out_ref.shape[-1]
    step = pl.program_id(0)
    odd_chip, odd_core, first_block = where_ref[0], where_ref[1], where_ref[2]
    starts = [0, HALO, HALO + rows, HALO + 2 * rows, HALO + 3 * rows]

    def copies(number, slot):
        whole = pl.ds(pl.multiple_of((first_block + number) * block, block), block)
        piece = pl.ds(pl.multiple_of(number * block, block), block)

        def one(source, part, count, index):
            return pltpu.make_async_copy(
                source, window.at[slot, starts[part] : starts[part] + count, :], sems.at[slot, index]
            )

        own = one(own_ref.at[:, whole], 2, rows, 2)
        core = (
            [one(near_ref.at[:, piece], 1, rows, 1), one(sibling_ref.at[:, whole], 3, rows, 3)],
            [one(sibling_ref.at[:, whole], 1, rows, 1), one(near_ref.at[:, piece], 3, rows, 3)],
        )
        last = slice(rows - HALO, rows)
        chip = (
            [one(onward_ref.at[last, piece], 0, HALO, 0), one(chip_ref.at[0:HALO, piece], 4, HALO, 4)],
            [one(chip_ref.at[last, piece], 0, HALO, 0), one(onward_ref.at[0:HALO, piece], 4, HALO, 4)],
        )
        return own, core, chip

    def begin(number, slot):
        own, core, chip = copies(number, slot)
        own.start()
        for odd in (0, 1):

            @pl.when(odd_core == odd)
            def _():
                core[odd][0].start()
                core[odd][1].start()

            @pl.when(odd_chip == odd)
            def _():
                chip[odd][0].start()
                chip[odd][1].start()

    @pl.when(step == 0)
    def _():
        begin(0, 0)

    slot = lax.rem(step, 2)

    @pl.when(step + 1 < steps)
    def _():
        begin(step + 1, 1 - slot)

    own, core, chip = copies(step, slot)
    own.wait()
    for copy in core[0] + chip[0]:
        copy.wait()

    def product(left, right):
        return jnp.dot(left, right, preferred_element_type=jnp.float32)

    for k in range(k_count):
        pair = pair_ref[k]
        lower = window[slot, 0:band, :]
        middle = window[slot, rows : rows + band, :]
        upper = window[slot, 2 * rows : 2 * rows + band, :]
        own_first = product(pair[:, 0:band], middle).astype(jnp.bfloat16)
        left_first = product(left_ref[k].reshape(2 * HALO, band), lower).astype(jnp.bfloat16)
        right_first = product(right_ref[k].reshape(2 * HALO, band), upper).astype(jnp.bfloat16)
        wide = jnp.concatenate(
            [
                piece
                for p in range(2)
                for piece in (
                    left_first[p * HALO : (p + 1) * HALO],
                    own_first[p * rows : (p + 1) * rows],
                    right_first[p * HALO : (p + 1) * HALO],
                )
            ],
            axis=0,
        )
        both = 2.0 * product(pair, wide)
        center = window[slot, HALO + rows : HALO + 2 * rows, :].astype(jnp.float32)
        out_ref[k, 0] = (both[0:rows] - center).astype(jnp.bfloat16)
        out_ref[k, 1] = both[rows:].astype(jnp.bfloat16)


def filter_columns(where, pair, left, right, own, sibling, near, chip, onward_rows, so_far):
    k_count, double_rows, _ = pair.shape
    rows = double_rows // 2
    columns = own.shape[1]
    block = min(BLOCK, near.shape[1])
    steps = near.shape[1] // block
    vmem = pl.BlockSpec(memory_space=pltpu.VMEM)
    hbm = pl.BlockSpec(memory_space=pl.ANY)
    operands = [where, pair, left, right, own, sibling, near, chip, onward_rows]
    specs = [vmem] * 3 + [hbm] * 5
    aliases = {}
    if so_far is not None:
        aliases = {len(operands): 0}
        operands.append(so_far)
        specs.append(hbm)
    return pl.pallas_call(
        functools.partial(filter_kernel, steps),
        out_shape=jax.ShapeDtypeStruct((k_count, 2, rows, columns), jnp.bfloat16),
        grid_spec=pltpu.PrefetchScalarGridSpec(
            num_scalar_prefetch=1,
            grid=(steps,),
            in_specs=specs,
            out_specs=pl.BlockSpec((k_count, 2, rows, block), lambda i, where: (0, 0, 0, where[2] + i)),
            scratch_shapes=[
                pltpu.VMEM((2, 3 * rows + 2 * HALO, block), jnp.bfloat16),
                pltpu.SemaphoreType.DMA((2, 5)),
            ],
        ),
        input_output_aliases=aliases,
        compiler_params=pltpu.CompilerParams(
            vmem_limit_bytes=40 * 1024 * 1024, dimension_semantics=("arbitrary",)
        ),
        cost_estimate=pl.CostEstimate(
            flops=2 * near.shape[1] * k_count * (4 * 256 * 256 + 2 * 192 * 256),
            bytes_accessed=near.shape[1] * 2 * (448 + 384),
            transcendentals=0,
        ),
        name="filter_columns",
    )(*operands)


def local(hopping_tiles, tile_strip, tile_column_slot, lattice, kpoints, start_block):
    owners = lax.axis_size("orb")
    device = lax.axis_index("orb")
    group = lax.axis_index("kgrp")
    odd_core = device & 1
    odd_chip = (device >> 1) & 1
    step_count, tile_count, row_count, col_width = hopping_tiles.shape
    slot_count = (row_count + 2 * HALO) // col_width
    k_count = kpoints.shape[0]
    half = start_block.shape[1] // 2
    piece = half // PIECES
    block = min(BLOCK, piece)

    dest_all = tile_strip[:, :, 0].reshape(owners, step_count, tile_count)
    own_dest = lax.dynamic_index_in_dim(dest_all, device, 0, keepdims=False).reshape(-1)
    tiles = hopping_tiles.reshape(step_count * tile_count, row_count, col_width)
    outgoing = pack_tiles(tiles, own_dest, owners)
    incoming = lax.all_to_all(outgoing, "orb", split_axis=0, concat_axis=0, tiled=True)
    phases = lax.optimization_barrier(phase_table(lattice, kpoints)).astype(jnp.float32)
    slot_all = tile_column_slot.reshape(owners, step_count, tile_count)
    weights = receive_weights(dest_all, slot_all, phases, device, slot_count)
    pair, tail, head = make_bands(weights, incoming, k_count, slot_count)
    left = shifted(tail, 1)
    right = shifted(head, -1)

    sibling = to_sibling(start_block)
    passes = odd_chip == odd_core
    result = None
    work = []
    for number in range(PIECES):
        begin = group * half + number * piece
        chip = to_pair_chip(lax.dynamic_slice_in_dim(start_block, begin, piece, axis=1))
        beyond = onward(chip)
        near = to_sibling(jnp.where(passes, chip, beyond))
        work.append((begin, near, chip, beyond))
        chip, beyond = to_other_group(chip), to_other_group(beyond)
        near = to_sibling(jnp.where(passes, chip, beyond))
        work.append(((1 - group) * half + number * piece, near, chip, beyond))
    for begin, near, chip, beyond in work:
        where = jnp.stack([odd_chip, odd_core, begin // block]).astype(jnp.int32)
        result = filter_columns(where, pair, left, right, start_block, sibling, near, chip, beyond, result)
    return result


def solution(mesh):
    return jax.shard_map(
        local,
        mesh=mesh,
        in_specs=(P("orb", None, None, None), P(), P(), P(), P("kgrp", None), P("orb", None)),
        out_specs=P("kgrp", None, "orb", None),
        check_vma=False,
    )
```

```python
import functools
import math

import jax
import jax.numpy as jnp
from jax import lax
from jax.experimental import pallas as pl
from jax.experimental.pallas import tpu as pltpu
from jax.sharding import PartitionSpec as P

HALO = 80
CAP = 2
LANES = 128
PIECES = 2
BLOCK = 1024


def routed(value, route):
    groups, owners = lax.axis_size("kgrp"), lax.axis_size("orb")
    pairs = []
    for group in range(groups):
        for owner in range(owners):
            to_group, to_owner = route(group, owner)
            if 0 <= to_owner < owners:
                pairs.append((group * owners + owner, to_group * owners + to_owner))
    return lax.ppermute(value, ("kgrp", "orb"), pairs)


def to_sibling(value):
    return routed(value, lambda group, owner: (group, owner ^ 1))


def to_pair_chip(value):
    return routed(value, lambda group, owner: (group, owner ^ 2))


def onward(value):
    return routed(value, lambda group, owner: (group, owner + (4 if owner & 2 == 0 else -4)))


def to_other_group(value):
    return routed(value, lambda group, owner: (1 - group, owner))


def shifted(value, steps):
    return routed(value, lambda group, owner: (group, owner + steps))


def after(value, *sooner):
    return lax.optimization_barrier((value,) + sooner)[0]


def pack_kernel(dest_ref, tiles_ref, packed_ref, placed, source):
    slots = packed_ref.shape[0]
    tile_count = dest_ref.shape[0]
    step_count = tiles_ref.shape[0] // tile_count
    first_vector = lax.axis_index("orb") * step_count

    def clear(slot, carry):
        source[slot] = 0
        return carry

    def forget(owner, carry):
        placed[owner] = 0
        return carry

    def place(tile, carry):
        dest = dest_ref[lax.rem(tile, tile_count), first_vector + tile // tile_count]
        rank = placed[dest]
        placed[dest] = rank + 1
        source[dest * CAP + rank] = tile
        return carry

    def fill(slot, carry):
        packed_ref[slot] = tiles_ref[source[slot]]
        return carry

    lax.fori_loop(0, slots, clear, 0, unroll=4)
    lax.fori_loop(0, slots // CAP, forget, 0, unroll=4)
    lax.fori_loop(0, step_count * tile_count, place, 0)
    lax.fori_loop(0, slots, fill, 0, unroll=2)


def pack_tiles(tiles, dest, owners):
    slots = owners * CAP
    vmem = pl.BlockSpec(memory_space=pltpu.VMEM)
    return pl.pallas_call(
        pack_kernel,
        out_shape=jax.ShapeDtypeStruct((slots,) + tiles.shape[1:], tiles.dtype),
        in_specs=[pl.BlockSpec(memory_space=pltpu.SMEM), vmem],
        out_specs=vmem,
        scratch_shapes=[pltpu.SMEM((owners,), jnp.int32), pltpu.SMEM((slots,), jnp.int32)],
        compiler_params=pltpu.CompilerParams(vmem_limit_bytes=40 * 1024 * 1024),
        name="pack_tiles",
    )(dest, tiles)


def weight_kernel(slot_count, point_ref, cell_ref, dest_ref, column_ref, weight_ref):
    tile_count, vectors = dest_ref.shape
    owners = weight_ref.shape[1] // LANES
    step_count = vectors // owners
    k_count = point_ref.shape[0]
    mine = dest_ref[...] == lax.axis_index("orb")
    flags = mine.astype(jnp.float32)
    shape = (tile_count, tile_count)
    before = lax.broadcasted_iota(jnp.int32, shape, 1) < lax.broadcasted_iota(jnp.int32, shape, 0)
    rank = jnp.dot(before.astype(jnp.float32), flags, preferred_element_type=jnp.float32)
    shape = (vectors, vectors)
    sooner, later = lax.broadcasted_iota(jnp.int32, shape, 0), lax.broadcasted_iota(jnp.int32, shape, 1)
    same_owner = (sooner < later) & (sooner >= later - later % step_count)
    counts = jnp.broadcast_to(jnp.sum(flags, axis=0, keepdims=True), (8, vectors))
    above = jnp.dot(counts, same_owner.astype(jnp.float32), preferred_element_type=jnp.float32)
    rank = (rank + above[0:1]).astype(jnp.int32)
    cells = cell_ref[...].astype(jnp.float32)
    column = column_ref[...]
    values = []
    for k in range(k_count):
        fraction = point_ref[k, 0] * cells[0:1] + point_ref[k, 1] * cells[1:2]
        fraction = fraction + point_ref[k, 2] * cells[2:3]
        radians = 6.283185307179586 * fraction
        for wave in (jnp.cos(radians), jnp.sin(radians)):
            phase = wave.astype(jnp.bfloat16).astype(jnp.float32)
            for j in range(slot_count):
                for c in range(CAP):
                    here = mine & (rank == c) & (column == j)
                    values.append(jnp.sum(jnp.where(here, phase, 0.0), axis=0, keepdims=True))
    values = jnp.concatenate(values, axis=0)
    chunk = math.gcd(owners, 16)
    shape = (vectors, chunk * LANES)
    for first in range(0, owners, chunk):
        owner = first + lax.broadcasted_iota(jnp.int32, shape, 1) // LANES
        member = (lax.broadcasted_iota(jnp.int32, shape, 0) // step_count == owner).astype(jnp.float32)
        weight_ref[:, first * LANES : (first + chunk) * LANES] = jnp.dot(
            values, member, preferred_element_type=jnp.float32
        )


def receive_weights(kpoints, cells, dest, column, owners, slot_count):
    k_count = kpoints.shape[0]
    smem, vmem = (pl.BlockSpec(memory_space=space) for space in (pltpu.SMEM, pltpu.VMEM))
    return pl.pallas_call(
        functools.partial(weight_kernel, slot_count),
        out_shape=jax.ShapeDtypeStruct((k_count * 2 * slot_count * CAP, owners * LANES), jnp.float32),
        in_specs=[smem, vmem, vmem, vmem],
        out_specs=vmem,
        compiler_params=pltpu.CompilerParams(vmem_limit_bytes=40 * 1024 * 1024),
        name="receive_weights",
    )(kpoints, cells, dest, column)


def band_kernel(k_count, slot_count, weight_ref, tiles_ref, pair_ref, tail_ref, head_ref):
    slots, rows, width = tiles_ref.shape
    part = rows // 2
    band = slot_count * width
    kinds = k_count * 2 * slot_count
    for low in (0, part):

        def add(owner, totals):
            lanes = pl.ds(pl.multiple_of(owner * LANES, LANES), LANES)
            for c in range(CAP):
                tile = tiles_ref[owner * CAP + c, low : low + part, :].astype(jnp.float32)
                totals = tuple(
                    total + weight_ref[pl.ds(kind * CAP + c, 1), lanes] * tile
                    for kind, total in enumerate(totals)
                )
            return totals

        totals = lax.fori_loop(
            0, slots // CAP, add, tuple(jnp.zeros((part, width), jnp.float32) for _ in range(kinds))
        )
        for k in range(k_count):
            for p in range(2):
                for j in range(slot_count):
                    value = totals[(k * 2 + p) * slot_count + j].astype(jnp.bfloat16)
                    columns = slice(j * width, (j + 1) * width)
                    later = slice(band + j * width, band + (j + 1) * width)
                    if p == 0:
                        pair_ref[k, low : low + part, columns] = value
                        pair_ref[k, rows + low : rows + low + part, later] = value
                    else:
                        pair_ref[k, rows + low : rows + low + part, columns] = value
                        pair_ref[k, low : low + part, later] = -value
    for k in range(k_count):
        for p in range(2):
            tail_ref[k, p] = pair_ref[k, (p + 1) * rows - HALO : (p + 1) * rows, 0:band]
            head_ref[k, p] = pair_ref[k, p * rows : p * rows + HALO, 0:band]


def make_bands(weights, tiles, k_count, slot_count):
    rows, width = tiles.shape[1:]
    band = slot_count * width
    vmem = pl.BlockSpec(memory_space=pltpu.VMEM)
    edge = jax.ShapeDtypeStruct((k_count, 2, HALO, band), jnp.bfloat16)
    return pl.pallas_call(
        functools.partial(band_kernel, k_count, slot_count),
        out_shape=[jax.ShapeDtypeStruct((k_count, 2 * rows, 2 * band), jnp.bfloat16), edge, edge],
        in_specs=[vmem, vmem],
        out_specs=[vmem, vmem, vmem],
        compiler_params=pltpu.CompilerParams(vmem_limit_bytes=40 * 1024 * 1024),
        name="make_bands",
    )(weights, tiles)


def filter_kernel(pieces, block_of, where_ref, pair_ref, left_ref, right_ref, own_ref, sibling_ref, *rest):
    chip_refs, onward_refs, near_refs = (rest[part * pieces : (part + 1) * pieces] for part in range(3))
    out_ref, window, sems = rest[-3:]
    k_count, double_rows, _ = pair_ref.shape
    rows = double_rows // 2
    band = left_ref.shape[-1]
    block = out_ref.shape[-1]
    piece_steps = chip_refs[0].shape[1] // block
    steps = pieces * piece_steps
    step = pl.program_id(0)
    odd_chip, odd_core, first_block = where_ref[0], where_ref[1], block_of(where_ref[2])
    starts = [0, HALO, HALO + rows, HALO + 2 * rows, HALO + 3 * rows]

    def begin(number, slot):
        whole = pl.ds(pl.multiple_of((first_block + number) * block, block), block)
        piece = pl.ds(pl.multiple_of(lax.rem(number, piece_steps) * block, block), block)

        def fetch(source, part):
            count = source.shape[0]
            pltpu.make_async_copy(
                source, window.at[slot, starts[part] : starts[part] + count, :], sems.at[slot, part]
            ).start()

        fetch(own_ref.at[:, whole], 2)
        for odd in (0, 1):

            @pl.when(odd_core == odd)
            def _():
                fetch(sibling_ref.at[:, whole], 1 if odd else 3)

            for index in range(pieces):
                inside = number // piece_steps == index

                @pl.when((odd_core == odd) & inside)
                def _():
                    fetch(near_refs[index].at[:, piece], 3 if odd else 1)

                @pl.when((odd_chip == odd) & inside)
                def _():
                    before, after = chip_refs[index], onward_refs[index]
                    if odd == 0:
                        before, after = after, before
                    fetch(before.at[rows - HALO : rows, piece], 0)
                    fetch(after.at[0:HALO, piece], 4)

    @pl.when(step == 0)
    def _():
        begin(0, 0)

    slot = lax.rem(step, 2)

    @pl.when(step + 1 < steps)
    def _():
        begin(step + 1, 1 - slot)

    for part in range(5):
        count = HALO if part in (0, 4) else rows
        target = window.at[slot, starts[part] : starts[part] + count, :]
        pltpu.make_async_copy(target, target, sems.at[slot, part]).wait()

    def product(left, right):
        return jnp.dot(left, right, preferred_element_type=jnp.float32)

    lower = window[slot, 0:band, :]
    middle = window[slot, rows : rows + band, :]
    upper = window[slot, 2 * rows : 2 * rows + band, :]
    own_band = jnp.concatenate([pair_ref[k][:, 0:band] for k in range(k_count)], axis=0)
    edges = k_count * 2 * HALO
    own_first = product(own_band, middle).astype(jnp.bfloat16)
    left_first = product(left_ref[...].reshape(edges, band), lower).astype(jnp.bfloat16)
    right_first = product(right_ref[...].reshape(edges, band), upper).astype(jnp.bfloat16)
    center = window[slot, HALO + rows : HALO + 2 * rows, :].astype(jnp.float32)
    for k in range(k_count):
        wide = jnp.concatenate(
            [
                part
                for kind in (2 * k, 2 * k + 1)
                for part in (
                    left_first[kind * HALO : (kind + 1) * HALO],
                    own_first[kind * rows : (kind + 1) * rows],
                    right_first[kind * HALO : (kind + 1) * HALO],
                )
            ],
            axis=0,
        )
        both = 2.0 * product(pair_ref[k], wide)
        out_ref[k, 0] = (both[0:rows] - center).astype(jnp.bfloat16)
        out_ref[k, 1] = both[rows:].astype(jnp.bfloat16)


def filter_columns(where, block_of, pair, left, right, own, sibling, halos, so_far):
    k_count, double_rows, _ = pair.shape
    rows = double_rows // 2
    columns = own.shape[1]
    pieces = len(halos)
    width = halos[0][0].shape[1]
    block = min(BLOCK, width)
    vmem = pl.BlockSpec(memory_space=pltpu.VMEM)
    hbm = pl.BlockSpec(memory_space=pltpu.HBM)
    operands = [where, pair, left, right, own, sibling]
    operands += [halo[part] for part in range(3) for halo in halos]
    specs = [vmem] * 3 + [hbm] * (2 + 3 * pieces)
    aliases = {}
    if so_far is not None:
        aliases = {len(operands): 0}
        operands.append(so_far)
        specs.append(hbm)
    return pl.pallas_call(
        functools.partial(filter_kernel, pieces, block_of),
        out_shape=jax.ShapeDtypeStruct((k_count, 2, rows, columns), jnp.bfloat16),
        grid_spec=pltpu.PrefetchScalarGridSpec(
            num_scalar_prefetch=1,
            grid=(pieces * width // block,),
            in_specs=specs,
            out_specs=pl.BlockSpec((k_count, 2, rows, block), lambda i, where: (0, 0, 0, block_of(where[2]) + i)),
            scratch_shapes=[
                pltpu.VMEM((2, 3 * rows + 2 * HALO, block), jnp.bfloat16),
                pltpu.SemaphoreType.DMA((2, 5)),
            ],
        ),
        input_output_aliases=aliases,
        compiler_params=pltpu.CompilerParams(
            vmem_limit_bytes=40 * 1024 * 1024, dimension_semantics=("arbitrary",)
        ),
        cost_estimate=pl.CostEstimate(
            flops=2 * pieces * width * k_count * (4 * 256 * 256 + 2 * 192 * 256),
            bytes_accessed=pieces * width * 2 * (448 + 384),
            transcendentals=0,
        ),
        name="filter_columns",
    )(*operands)


def local(hopping_tiles, tile_strip, tile_column_slot, lattice, kpoints, start_block):
    owners = lax.axis_size("orb")
    device = lax.axis_index("orb")
    group = lax.axis_index("kgrp")
    odd_core = device & 1
    odd_chip = (device >> 1) & 1
    step_count, tile_count, row_count, col_width = hopping_tiles.shape
    slot_count = (row_count + 2 * HALO) // col_width
    k_count = kpoints.shape[0]
    half = start_block.shape[1] // 2
    piece = half // PIECES
    block = min(BLOCK, piece)

    dest = jnp.transpose(tile_strip, (2, 1, 0))[0]
    tiles = hopping_tiles.reshape(step_count * tile_count, row_count, col_width)
    outgoing = pack_tiles(tiles, dest, owners)
    incoming = lax.all_to_all(outgoing, "orb", split_axis=0, concat_axis=0, tiled=True)
    weights = receive_weights(kpoints, lattice.T, dest, tile_column_slot.T, owners, slot_count)

    chips, beyonds = [], []
    for number in range(PIECES):
        source = after(start_block, *chips[-1:])
        chip = to_pair_chip(lax.dynamic_slice_in_dim(source, group * half + number * piece, piece, axis=1))
        chips.append(after(chip, outgoing))
        beyonds.append(onward(chips[-1]))
    other_chips = [to_other_group(chip) for chip in chips]

    pair, tail, head = make_bands(weights, after(incoming, *other_chips), k_count, slot_count)
    left = shifted(tail, 1)
    right = shifted(head, -1)

    sibling = to_sibling(start_block)
    where = jnp.stack([odd_chip, odd_core, group]).astype(jnp.int32)

    def filtered(other, halos, so_far):
        return filter_columns(
            where,
            lambda group: (group + other - 2 * group * other) * (half // block),
            pair,
            left,
            right,
            start_block,
            sibling,
            halos,
            so_far,
        )

    passes = odd_chip == odd_core

    def to_near(chip, beyond):
        return to_sibling(jnp.where(passes, chip, beyond))

    beyonds[-1] = after(beyonds[-1], pair)
    other_beyonds = [to_other_group(beyond) for beyond in beyonds]
    nears = [to_near(chip, beyond) for chip, beyond in zip(chips, beyonds)]
    nears[0] = after(nears[0], *other_beyonds[:-1])
    result = filtered(0, list(zip(chips, beyonds, nears)), None)
    other_beyonds = [after(beyond, result) for beyond in other_beyonds]
    other_nears = [to_near(chip, beyond) for chip, beyond in zip(other_chips, other_beyonds)]
    return filtered(1, list(zip(other_chips, other_beyonds, other_nears)), result)


def solution(mesh):
    return jax.shard_map(
        local,
        mesh=mesh,
        in_specs=(P("orb", None, None, None), P(), P(), P(), P("kgrp", None), P("orb", None)),
        out_specs=P("kgrp", None, "orb", None),
        check_vma=False,
    )
```

```python
import functools
import math

import jax
import jax.numpy as jnp
from jax import lax
from jax.experimental import pallas as pl
from jax.experimental.pallas import tpu as pltpu
from jax.sharding import PartitionSpec as P

HALO = 80
CAP = 2
LANES = 128
MUCH = 60 << 20
LITTLE = 32 << 20
BLOCK = 1024


def routed(value, route):
    groups, owners = lax.axis_size("kgrp"), lax.axis_size("orb")
    pairs = []
    for group in range(groups):
        for owner in range(owners):
            to_group, to_owner = route(group, owner)
            if 0 <= to_owner < owners:
                pairs.append((group * owners + owner, to_group * owners + to_owner))
    return lax.ppermute(value, ("kgrp", "orb"), pairs)


def to_sibling(value):
    return routed(value, lambda group, owner: (group, owner ^ 1))


def to_pair_chip(value):
    return routed(value, lambda group, owner: (group, owner ^ 2))


def onward(value):
    return routed(value, lambda group, owner: (group, owner + (4 if owner & 2 == 0 else -4)))


def to_other_group(value):
    return routed(value, lambda group, owner: (1 - group, owner))


def to_next_chip(value):
    return routed(value, lambda group, owner: (group, owner + (1 if owner & 1 else -1)))


def after(value, *sooner):
    return lax.optimization_barrier((value,) + sooner)[0]


def pack_kernel(dest_ref, tiles_ref, packed_ref, placed, source):
    slots = packed_ref.shape[0]
    tile_count = dest_ref.shape[0]
    step_count = tiles_ref.shape[0] // tile_count
    first_vector = lax.axis_index("orb") * step_count
    part = packed_ref.shape[1]
    rows = pl.ds(pl.multiple_of(lax.axis_index("kgrp") * part, part), part)

    def clear(slot, carry):
        source[slot] = 0
        return carry

    def forget(owner, carry):
        placed[owner] = 0
        return carry

    def place(tile, carry):
        dest = dest_ref[lax.rem(tile, tile_count), 0, first_vector + tile // tile_count]
        rank = placed[dest]
        placed[dest] = rank + 1
        source[dest * CAP + rank] = tile
        return carry

    def fill(slot, carry):
        packed_ref[slot] = tiles_ref[source[slot], rows, :]
        return carry

    lax.fori_loop(0, slots, clear, 0, unroll=4)
    lax.fori_loop(0, slots // CAP, forget, 0, unroll=4)
    lax.fori_loop(0, step_count * tile_count, place, 0)
    lax.fori_loop(0, slots, fill, 0, unroll=2)


def pack_tiles(tiles, dest, owners):
    slots = owners * CAP
    rows, width = tiles.shape[1:]
    vmem = pl.BlockSpec(memory_space=pltpu.VMEM)
    return pl.pallas_call(
        pack_kernel,
        out_shape=jax.ShapeDtypeStruct((slots, rows // lax.axis_size("kgrp"), width), tiles.dtype),
        in_specs=[pl.BlockSpec(memory_space=pltpu.SMEM), vmem],
        out_specs=vmem,
        scratch_shapes=[pltpu.SMEM((owners,), jnp.int32), pltpu.SMEM((slots,), jnp.int32)],
        compiler_params=pltpu.CompilerParams(vmem_limit_bytes=MUCH),
        cost_estimate=pl.CostEstimate(flops=0, bytes_accessed=0, transcendentals=0),
        name="pack_tiles",
    )(dest, tiles)


def weight_kernel(slot_count, *refs):
    sources, (weight_ref, point_ref, cell_ref, dest_ref, column_ref, sems) = refs[:4], refs[4:]
    copies = [
        pltpu.make_async_copy(source, target, sems.at[index])
        for index, (source, target) in enumerate(zip(sources, (point_ref, cell_ref, dest_ref, column_ref)))
    ]
    for copy in copies:
        copy.start()
    for copy in copies:
        copy.wait()
    tile_count, _, vectors = dest_ref.shape
    owners = weight_ref.shape[1] // LANES
    step_count = vectors // owners
    k_count = point_ref.shape[0]
    mine = dest_ref[:, 0, :] == lax.axis_index("orb")
    flags = mine.astype(jnp.float32)
    shape = (tile_count, tile_count)
    before = lax.broadcasted_iota(jnp.int32, shape, 1) < lax.broadcasted_iota(jnp.int32, shape, 0)
    rank = jnp.dot(before.astype(jnp.float32), flags, preferred_element_type=jnp.float32)
    shape = (vectors, vectors)
    sooner, later = lax.broadcasted_iota(jnp.int32, shape, 0), lax.broadcasted_iota(jnp.int32, shape, 1)
    same_owner = (sooner < later) & (sooner >= later - later % step_count)
    counts = jnp.broadcast_to(jnp.sum(flags, axis=0, keepdims=True), (8, vectors))
    above = jnp.dot(counts, same_owner.astype(jnp.float32), preferred_element_type=jnp.float32)
    rank = (rank + above[0:1]).astype(jnp.int32)
    cells = cell_ref[...].astype(jnp.float32)
    column = column_ref[...]
    values = []
    for k in range(k_count):
        fraction = point_ref[k, 0] * cells[0:1] + point_ref[k, 1] * cells[1:2]
        fraction = fraction + point_ref[k, 2] * cells[2:3]
        radians = 6.283185307179586 * fraction
        for wave in (jnp.cos(radians), jnp.sin(radians)):
            phase = wave.astype(jnp.bfloat16).astype(jnp.float32)
            for j in range(slot_count):
                for c in range(CAP):
                    here = mine & (rank == c) & (column == j)
                    values.append(jnp.sum(jnp.where(here, phase, 0.0), axis=0, keepdims=True))
    values = jnp.concatenate(values, axis=0)
    chunk = math.gcd(owners, 16)
    shape = (vectors, chunk * LANES)
    for first in range(0, owners, chunk):
        owner = first + lax.broadcasted_iota(jnp.int32, shape, 1) // LANES
        member = (lax.broadcasted_iota(jnp.int32, shape, 0) // step_count == owner).astype(jnp.float32)
        weight_ref[:, first * LANES : (first + chunk) * LANES] = jnp.dot(
            values, member, preferred_element_type=jnp.float32
        )


def receive_weights(kpoints, cells, dest, column, owners, slot_count):
    k_count = kpoints.shape[0]
    operands = (kpoints, cells, dest, column)
    spaces = (pltpu.SMEM, pltpu.VMEM, pltpu.VMEM, pltpu.VMEM)
    return pl.pallas_call(
        functools.partial(weight_kernel, slot_count),
        out_shape=jax.ShapeDtypeStruct((k_count * 2 * slot_count * CAP, owners * LANES), jnp.float32),
        in_specs=[pl.BlockSpec(memory_space=pltpu.HBM)] * 4,
        out_specs=pl.BlockSpec(memory_space=pltpu.VMEM),
        scratch_shapes=[space(array.shape, array.dtype) for space, array in zip(spaces, operands)]
        + [pltpu.SemaphoreType.DMA((4,))],
        compiler_params=pltpu.CompilerParams(vmem_limit_bytes=LITTLE),
        cost_estimate=pl.CostEstimate(flops=0, bytes_accessed=0, transcendentals=0),
        name="receive_weights",
    )(*operands)


def add_tiles(weight_ref, tiles_ref, pair_ref, index, k_count, slot_count):
    slots, part, width = tiles_ref.shape
    rows = pair_ref.shape[1] // 2
    band = slot_count * width
    kinds = k_count * 2 * slot_count

    def add(owner, totals):
        lanes = pl.ds(pl.multiple_of(owner * LANES, LANES), LANES)
        for c in range(CAP):
            tile = tiles_ref[owner * CAP + c].astype(jnp.float32)
            totals = tuple(
                total + weight_ref[pl.ds(kind * CAP + c, 1), lanes] * tile for kind, total in enumerate(totals)
            )
        return totals

    totals = lax.fori_loop(
        0, slots // CAP, add, tuple(jnp.zeros((part, width), jnp.float32) for _ in range(kinds))
    )
    top = pl.ds(pl.multiple_of(index * part, part), part)
    bottom = pl.ds(pl.multiple_of(rows + index * part, part), part)
    for k in range(k_count):
        for p in range(2):
            for j in range(slot_count):
                value = totals[(k * 2 + p) * slot_count + j].astype(jnp.bfloat16)
                columns = slice(j * width, (j + 1) * width)
                later = slice(band + j * width, band + (j + 1) * width)
                if p == 0:
                    pair_ref[k, top, columns] = value
                    pair_ref[k, bottom, later] = value
                else:
                    pair_ref[k, bottom, columns] = value
                    pair_ref[k, top, later] = -value


def begin_kernel(k_count, slot_count, weight_ref, tiles_ref, pair_ref):
    add_tiles(weight_ref, tiles_ref, pair_ref, lax.axis_index("kgrp"), k_count, slot_count)


def band_kernel(k_count, slot_count, weight_ref, tiles_ref, begun_ref, pair_ref, core_ref, chip_ref):
    rows = pair_ref.shape[1] // 2
    band = core_ref.shape[-1]
    pair_ref[...] = begun_ref[...]
    add_tiles(weight_ref, tiles_ref, pair_ref, 1 - lax.axis_index("kgrp"), k_count, slot_count)
    odd_core = lax.axis_index("orb") & 1
    for odd in (0, 1):

        @pl.when(odd_core == odd)
        def _():
            tail_ref, head_ref = (chip_ref, core_ref) if odd else (core_ref, chip_ref)
            for k in range(k_count):
                for p in range(2):
                    tail_ref[k, p] = pair_ref[k, (p + 1) * rows - HALO : (p + 1) * rows, 0:band]
                    head_ref[k, p] = pair_ref[k, p * rows : p * rows + HALO, 0:band]


def begin_bands(weights, tiles, k_count, slot_count):
    part, width = tiles.shape[1:]
    vmem = pl.BlockSpec(memory_space=pltpu.VMEM)
    return pl.pallas_call(
        functools.partial(begin_kernel, k_count, slot_count),
        out_shape=jax.ShapeDtypeStruct((k_count, 4 * part, 2 * slot_count * width), jnp.bfloat16),
        in_specs=[vmem, vmem],
        out_specs=vmem,
        compiler_params=pltpu.CompilerParams(vmem_limit_bytes=LITTLE),
        cost_estimate=pl.CostEstimate(flops=0, bytes_accessed=0, transcendentals=0),
        name="begin_bands",
    )(weights, tiles)


def make_bands(weights, tiles, begun, k_count, slot_count):
    band = slot_count * tiles.shape[2]
    edge = (k_count, 2, HALO, band)
    vmem = pl.BlockSpec(memory_space=pltpu.VMEM)
    return pl.pallas_call(
        functools.partial(band_kernel, k_count, slot_count),
        out_shape=[jax.ShapeDtypeStruct(shape, jnp.bfloat16) for shape in (begun.shape, edge, edge)],
        in_specs=[vmem, vmem, vmem],
        out_specs=[vmem, vmem, vmem],
        compiler_params=pltpu.CompilerParams(vmem_limit_bytes=LITTLE),
        cost_estimate=pl.CostEstimate(flops=0, bytes_accessed=0, transcendentals=0),
        name="make_bands",
    )(weights, tiles, begun)


def filter_kernel(places, pair_ref, core_ref, chip_ref, own_ref, sibling_ref, *rest):
    pieces = len(places)
    chip_refs, onward_refs, near_chip_refs, near_onward_refs = (
        rest[part * pieces : (part + 1) * pieces] for part in range(4)
    )
    result_ref, window, done, edges, sems, done_sems = rest[-6:]
    chunks, _, block = window.shape
    k_count, double_rows, _ = pair_ref.shape
    rows = double_rows // 2
    band = core_ref.shape[-1]
    per_piece = chunks // pieces
    group = lax.axis_index("kgrp")
    state = lax.axis_index("orb") & 3
    starts = [0, HALO, HALO + rows, HALO + 2 * rows, HALO + 3 * rows]

    def columns_of(chunk):
        fixed, by_group = places[chunk // per_piece]
        first = fixed + by_group * group + chunk % per_piece * block
        return pl.ds(pl.multiple_of(first, block), block)

    for odd_chip in (0, 1):
        for odd_core in (0, 1):

            @pl.when(state == odd_chip * 2 + odd_core)
            def _():
                for chunk in range(chunks):
                    whole = columns_of(chunk)
                    index, place = chunk // per_piece, chunk % per_piece
                    piece = pl.ds(place * block, block)
                    sibling = sibling_ref.at[:, whole]
                    near = (near_onward_refs if odd_chip == odd_core else near_chip_refs)[index].at[:, piece]
                    before, beyond = chip_refs[index], onward_refs[index]
                    if odd_chip == 0:
                        before, beyond = beyond, before
                    sources = [
                        before.at[rows - HALO : rows, piece],
                        sibling if odd_core else near,
                        own_ref.at[:, whole],
                        near if odd_core else sibling,
                        beyond.at[0:HALO, piece],
                    ]
                    for part, source in enumerate(sources):
                        count = source.shape[0]
                        target = window.at[chunk, starts[part] : starts[part] + count, :]
                        pltpu.make_async_copy(source, target, sems.at[chunk, part]).start()
                edges[1 - odd_core] = core_ref[...]
                edges[odd_core] = chip_ref[...]

    def product(left, right):
        return jnp.dot(left, right, preferred_element_type=jnp.float32)

    own_band = jnp.concatenate([pair_ref[k][:, 0:band] for k in range(k_count)], axis=0)
    halo_rows = k_count * 2 * HALO

    def result_copy(chunk):
        return pltpu.make_async_copy(
            done.at[chunk], result_ref.at[:, :, :, columns_of(chunk)], done_sems.at[chunk]
        )

    for chunk in range(chunks):
        for part in range(5):
            count = HALO if part in (0, 4) else rows
            target = window.at[chunk, starts[part] : starts[part] + count, :]
            pltpu.make_async_copy(target, target, sems.at[chunk, part]).wait()
        lower = window[chunk, 0:band, :]
        middle = window[chunk, rows : rows + band, :]
        upper = window[chunk, 2 * rows : 2 * rows + band, :]
        own_first = product(own_band, middle).astype(jnp.bfloat16)
        left_first = product(edges[0].reshape(halo_rows, band), lower).astype(jnp.bfloat16)
        right_first = product(edges[1].reshape(halo_rows, band), upper).astype(jnp.bfloat16)
        center = window[chunk, HALO + rows : HALO + 2 * rows, :].astype(jnp.float32)
        for k in range(k_count):
            wide = jnp.concatenate(
                [
                    part
                    for kind in (2 * k, 2 * k + 1)
                    for part in (
                        left_first[kind * HALO : (kind + 1) * HALO],
                        own_first[kind * rows : (kind + 1) * rows],
                        right_first[kind * HALO : (kind + 1) * HALO],
                    )
                ],
                axis=0,
            )
            both = 2.0 * product(pair_ref[k], wide)
            done[chunk, k, 0] = (both[0:rows] - center).astype(jnp.bfloat16)
            done[chunk, k, 1] = both[rows:].astype(jnp.bfloat16)
        result_copy(chunk).start()
    for chunk in range(chunks):
        result_copy(chunk).wait()


def filter_columns(places, pair, core_band, chip_band, own, sibling, halos, so_far):
    k_count, double_rows, _ = pair.shape
    rows = double_rows // 2
    columns = own.shape[1]
    pieces = len(halos)
    width = halos[0][0].shape[1]
    block = min(BLOCK, width)
    chunks = pieces * width // block
    vmem = pl.BlockSpec(memory_space=pltpu.VMEM)
    hbm = pl.BlockSpec(memory_space=pltpu.HBM)
    operands = [pair, core_band, chip_band, own, sibling]
    operands += [halo[part] for part in range(4) for halo in halos]
    specs = [vmem] * 3 + [hbm] * (2 + 4 * pieces)
    aliases = {}
    if so_far is not None:
        aliases = {len(operands): 0}
        operands.append(so_far)
        specs.append(hbm)
    return pl.pallas_call(
        functools.partial(filter_kernel, places),
        out_shape=jax.ShapeDtypeStruct((k_count, 2, rows, columns), jnp.bfloat16),
        in_specs=specs,
        out_specs=hbm,
        scratch_shapes=[
            pltpu.VMEM((chunks, 3 * rows + 2 * HALO, block), jnp.bfloat16),
            pltpu.VMEM((chunks, k_count, 2, rows, block), jnp.bfloat16),
            pltpu.VMEM((2,) + core_band.shape, jnp.bfloat16),
            pltpu.SemaphoreType.DMA((chunks, 5)),
            pltpu.SemaphoreType.DMA((chunks,)),
        ],
        input_output_aliases=aliases,
        compiler_params=pltpu.CompilerParams(vmem_limit_bytes=MUCH),
        cost_estimate=pl.CostEstimate(
            flops=0,
            bytes_accessed=0,
            transcendentals=0,
        ),
        name="filter_columns",
    )(*operands)


def local(hopping_tiles, tile_strip, tile_column_slot, lattice, kpoints, start_block):
    owners = lax.axis_size("orb")
    group = lax.axis_index("kgrp")
    step_count, tile_count, row_count, col_width = hopping_tiles.shape
    slot_count = (row_count + 2 * HALO) // col_width
    k_count = kpoints.shape[0]
    piece = start_block.shape[1] // 4

    dest = jnp.transpose(tile_strip, (1, 2, 0))
    tiles = hopping_tiles.reshape(step_count * tile_count, row_count, col_width)
    outgoing = pack_tiles(tiles, dest, owners)
    weights = receive_weights(kpoints, lattice.T, dest, tile_column_slot.T, owners, slot_count)
    incoming = lax.all_to_all(outgoing, "orb", split_axis=0, concat_axis=0, tiled=True)

    shared = to_pair_chip(lax.dynamic_slice_in_dim(start_block, group * piece, piece, axis=1))
    shared = after(shared, outgoing)
    third = to_pair_chip(after(start_block, shared)[:, 2 * piece : 3 * piece])
    other = to_other_group(shared)
    near_shared = to_sibling(shared)
    sibling = to_sibling(start_block)
    shared_beyond = onward(shared)

    begun = begin_bands(weights, after(incoming, other, near_shared, sibling), k_count, slot_count)
    theirs = to_other_group(after(incoming, begun))
    third = after(third, begun)
    fourth = to_pair_chip(after(start_block, third)[:, 3 * piece : 4 * piece])
    third_beyond = onward(third)
    begun = after(begun, shared_beyond)
    pair, for_core, for_chip = make_bands(weights, theirs, begun, k_count, slot_count)
    core_band, chip_band = to_sibling(for_core), to_next_chip(for_chip)

    swapped = (core_band, chip_band)
    fourth = after(fourth, *swapped)
    shared_beyond, third_beyond = after(shared_beyond, *swapped), after(third_beyond, fourth)
    near_shared_beyond, near_third_beyond = to_sibling(shared_beyond), to_sibling(third_beyond)
    near_third, near_other = to_sibling(after(third, pair)), to_sibling(after(other, pair))
    other_beyond = to_other_group(shared_beyond)
    fourth_beyond = onward(fourth)
    near_fourth = to_sibling(fourth)

    def filtered(places, halos, so_far):
        return filter_columns(places, pair, core_band, chip_band, start_block, sibling, halos, so_far)

    result = filtered(
        [(0, piece), (2 * piece, 0)],
        [
            (shared, shared_beyond, near_shared, near_shared_beyond),
            (third, third_beyond, near_third, near_third_beyond),
        ],
        None,
    )
    other_beyond, fourth_beyond = after(other_beyond, result), after(fourth_beyond, result)
    return filtered(
        [(piece, -piece), (3 * piece, 0)],
        [
            (other, other_beyond, near_other, to_sibling(other_beyond)),
            (fourth, fourth_beyond, near_fourth, to_sibling(fourth_beyond)),
        ],
        result,
    )


def solution(mesh):
    return jax.shard_map(
        local,
        mesh=mesh,
        in_specs=(P("orb", None, None, None), P(), P(), P(), P("kgrp", None), P("orb", None)),
        out_specs=P("kgrp", None, "orb", None),
        check_vma=False,
    )
```

```python
import functools
import math

import jax
import jax.numpy as jnp
from jax import lax
from jax.experimental import pallas as pl
from jax.experimental.pallas import tpu as pltpu
from jax.sharding import PartitionSpec as P

HALO = 80
CAP = 2
LANES = 128
MUCH = 60 << 20
LITTLE = 32 << 20
BLOCK = 1024


def routed(value, route):
    groups, owners = lax.axis_size("kgrp"), lax.axis_size("orb")
    pairs = []
    for group in range(groups):
        for owner in range(owners):
            to_group, to_owner = route(group, owner)
            if 0 <= to_owner < owners:
                pairs.append((group * owners + owner, to_group * owners + to_owner))
    return lax.ppermute(value, ("kgrp", "orb"), pairs)


def to_sibling(value):
    return routed(value, lambda group, owner: (group, owner ^ 1))


def to_pair_chip(value):
    return routed(value, lambda group, owner: (group, owner ^ 2))


def onward(value):
    return routed(value, lambda group, owner: (group, owner + (4 if owner & 2 == 0 else -4)))


def to_other_group(value):
    return routed(value, lambda group, owner: (1 - group, owner))


def to_next_chip(value):
    return routed(value, lambda group, owner: (group, owner + (1 if owner & 1 else -1)))


def after(value, *sooner):
    return lax.optimization_barrier((value,) + sooner)[0]


def pack_kernel(dest_ref, tiles_ref, packed_ref, placed, source):
    slots = packed_ref.shape[0]
    tile_count = dest_ref.shape[0]
    step_count = tiles_ref.shape[0] // tile_count
    first_vector = lax.axis_index("orb") * step_count
    part = packed_ref.shape[1]
    rows = pl.ds(pl.multiple_of(lax.axis_index("kgrp") * part, part), part)

    def clear(slot, carry):
        source[slot] = 0
        return carry

    def forget(owner, carry):
        placed[owner] = 0
        return carry

    def place(tile, carry):
        dest = dest_ref[lax.rem(tile, tile_count), 0, first_vector + tile // tile_count]
        rank = placed[dest]
        placed[dest] = rank + 1
        source[dest * CAP + rank] = tile
        return carry

    def fill(slot, carry):
        packed_ref[slot] = tiles_ref[source[slot], rows, :]
        return carry

    lax.fori_loop(0, slots, clear, 0, unroll=4)
    lax.fori_loop(0, slots // CAP, forget, 0, unroll=4)
    lax.fori_loop(0, step_count * tile_count, place, 0)
    lax.fori_loop(0, slots, fill, 0, unroll=2)


def pack_tiles(tiles, dest, owners):
    slots = owners * CAP
    rows, width = tiles.shape[1:]
    vmem = pl.BlockSpec(memory_space=pltpu.VMEM)
    return pl.pallas_call(
        pack_kernel,
        out_shape=jax.ShapeDtypeStruct((slots, rows // lax.axis_size("kgrp"), width), tiles.dtype),
        in_specs=[pl.BlockSpec(memory_space=pltpu.SMEM), vmem],
        out_specs=vmem,
        scratch_shapes=[pltpu.SMEM((owners,), jnp.int32), pltpu.SMEM((slots,), jnp.int32)],
        compiler_params=pltpu.CompilerParams(vmem_limit_bytes=MUCH),
        cost_estimate=pl.CostEstimate(flops=0, bytes_accessed=0, transcendentals=0),
        name="pack_tiles",
    )(dest, tiles)


def weight_kernel(slot_count, *refs):
    sources, (weight_ref, point_ref, cell_ref, dest_ref, column_ref, sems) = refs[:4], refs[4:]
    copies = [
        pltpu.make_async_copy(source, target, sems.at[index])
        for index, (source, target) in enumerate(zip(sources, (point_ref, cell_ref, dest_ref, column_ref)))
    ]
    for copy in copies:
        copy.start()
    for copy in copies:
        copy.wait()
    tile_count, _, vectors = dest_ref.shape
    owners = weight_ref.shape[1] // LANES
    step_count = vectors // owners
    k_count = point_ref.shape[0]
    mine = dest_ref[:, 0, :] == lax.axis_index("orb")
    flags = mine.astype(jnp.float32)
    shape = (tile_count, tile_count)
    before = lax.broadcasted_iota(jnp.int32, shape, 1) < lax.broadcasted_iota(jnp.int32, shape, 0)
    rank = jnp.dot(before.astype(jnp.float32), flags, preferred_element_type=jnp.float32)
    shape = (vectors, vectors)
    sooner, later = lax.broadcasted_iota(jnp.int32, shape, 0), lax.broadcasted_iota(jnp.int32, shape, 1)
    same_owner = (sooner < later) & (sooner >= later - later % step_count)
    counts = jnp.broadcast_to(jnp.sum(flags, axis=0, keepdims=True), (8, vectors))
    above = jnp.dot(counts, same_owner.astype(jnp.float32), preferred_element_type=jnp.float32)
    rank = (rank + above[0:1]).astype(jnp.int32)
    cells = cell_ref[...].astype(jnp.float32)
    column = column_ref[...]
    values = []
    for k in range(k_count):
        fraction = point_ref[k, 0] * cells[0:1] + point_ref[k, 1] * cells[1:2]
        fraction = fraction + point_ref[k, 2] * cells[2:3]
        radians = 6.283185307179586 * fraction
        for wave in (jnp.cos(radians), jnp.sin(radians)):
            phase = wave.astype(jnp.bfloat16).astype(jnp.float32)
            for j in range(slot_count):
                for c in range(CAP):
                    here = mine & (rank == c) & (column == j)
                    values.append(jnp.sum(jnp.where(here, phase, 0.0), axis=0, keepdims=True))
    values = jnp.concatenate(values, axis=0)
    chunk = math.gcd(owners, 16)
    shape = (vectors, chunk * LANES)
    for first in range(0, owners, chunk):
        owner = first + lax.broadcasted_iota(jnp.int32, shape, 1) // LANES
        member = (lax.broadcasted_iota(jnp.int32, shape, 0) // step_count == owner).astype(jnp.float32)
        weight_ref[:, first * LANES : (first + chunk) * LANES] = jnp.dot(
            values, member, preferred_element_type=jnp.float32
        )


def receive_weights(kpoints, cells, dest, column, owners, slot_count):
    k_count = kpoints.shape[0]
    operands = (kpoints, cells, dest, column)
    spaces = (pltpu.SMEM, pltpu.VMEM, pltpu.VMEM, pltpu.VMEM)
    return pl.pallas_call(
        functools.partial(weight_kernel, slot_count),
        out_shape=jax.ShapeDtypeStruct((k_count * 2 * slot_count * CAP, owners * LANES), jnp.float32),
        in_specs=[pl.BlockSpec(memory_space=pltpu.HBM)] * 4,
        out_specs=pl.BlockSpec(memory_space=pltpu.VMEM),
        scratch_shapes=[space(array.shape, array.dtype) for space, array in zip(spaces, operands)]
        + [pltpu.SemaphoreType.DMA((4,))],
        compiler_params=pltpu.CompilerParams(vmem_limit_bytes=LITTLE),
        cost_estimate=pl.CostEstimate(flops=0, bytes_accessed=0, transcendentals=0),
        name="receive_weights",
    )(*operands)


def add_tiles(weight_ref, tiles_ref, pair_ref, index, k_count, slot_count):
    slots, part, width = tiles_ref.shape
    rows = pair_ref.shape[1] // 2
    band = slot_count * width
    kinds = k_count * 2 * slot_count

    def add(owner, totals):
        lanes = pl.ds(pl.multiple_of(owner * LANES, LANES), LANES)
        for c in range(CAP):
            tile = tiles_ref[owner * CAP + c].astype(jnp.float32)
            totals = tuple(
                total + weight_ref[pl.ds(kind * CAP + c, 1), lanes] * tile for kind, total in enumerate(totals)
            )
        return totals

    totals = lax.fori_loop(
        0, slots // CAP, add, tuple(jnp.zeros((part, width), jnp.float32) for _ in range(kinds))
    )
    top = pl.ds(pl.multiple_of(index * part, part), part)
    bottom = pl.ds(pl.multiple_of(rows + index * part, part), part)
    for k in range(k_count):
        for p in range(2):
            for j in range(slot_count):
                value = totals[(k * 2 + p) * slot_count + j].astype(jnp.bfloat16)
                columns = slice(j * width, (j + 1) * width)
                later = slice(band + j * width, band + (j + 1) * width)
                if p == 0:
                    pair_ref[k, top, columns] = value
                    pair_ref[k, bottom, later] = value
                else:
                    pair_ref[k, bottom, columns] = value
                    pair_ref[k, top, later] = -value


def begin_kernel(k_count, slot_count, weight_ref, tiles_ref, pair_ref):
    add_tiles(weight_ref, tiles_ref, pair_ref, lax.axis_index("kgrp"), k_count, slot_count)


def band_kernel(k_count, slot_count, weight_ref, tiles_ref, begun_ref, pair_ref, core_ref, chip_ref):
    rows = pair_ref.shape[1] // 2
    band = core_ref.shape[-1]
    pair_ref[...] = begun_ref[...]
    add_tiles(weight_ref, tiles_ref, pair_ref, 1 - lax.axis_index("kgrp"), k_count, slot_count)
    odd_core = lax.axis_index("orb") & 1
    for odd in (0, 1):

        @pl.when(odd_core == odd)
        def _():
            tail_ref, head_ref = (chip_ref, core_ref) if odd else (core_ref, chip_ref)
            for k in range(k_count):
                for p in range(2):
                    tail_ref[k, p] = pair_ref[k, (p + 1) * rows - HALO : (p + 1) * rows, 0:band]
                    head_ref[k, p] = pair_ref[k, p * rows : p * rows + HALO, 0:band]


def begin_bands(weights, tiles, k_count, slot_count):
    part, width = tiles.shape[1:]
    vmem = pl.BlockSpec(memory_space=pltpu.VMEM)
    return pl.pallas_call(
        functools.partial(begin_kernel, k_count, slot_count),
        out_shape=jax.ShapeDtypeStruct((k_count, 4 * part, 2 * slot_count * width), jnp.bfloat16),
        in_specs=[vmem, vmem],
        out_specs=vmem,
        compiler_params=pltpu.CompilerParams(vmem_limit_bytes=LITTLE),
        cost_estimate=pl.CostEstimate(flops=0, bytes_accessed=0, transcendentals=0),
        name="begin_bands",
    )(weights, tiles)


def make_bands(weights, tiles, begun, k_count, slot_count):
    band = slot_count * tiles.shape[2]
    edge = (k_count, 2, HALO, band)
    vmem = pl.BlockSpec(memory_space=pltpu.VMEM)
    return pl.pallas_call(
        functools.partial(band_kernel, k_count, slot_count),
        out_shape=[jax.ShapeDtypeStruct(shape, jnp.bfloat16) for shape in (begun.shape, edge, edge)],
        in_specs=[vmem, vmem, vmem],
        out_specs=[vmem, vmem, vmem],
        compiler_params=pltpu.CompilerParams(vmem_limit_bytes=LITTLE),
        cost_estimate=pl.CostEstimate(flops=0, bytes_accessed=0, transcendentals=0),
        name="make_bands",
    )(weights, tiles, begun)


def filter_kernel(places, pair_source, core_ref, chip_ref, own_ref, sibling_ref, *rest):
    pieces = len(places)
    chip_refs, onward_refs, near_chip_refs, near_onward_refs = (
        rest[part * pieces : (part + 1) * pieces] for part in range(4)
    )
    result_ref, pair_ref, window, done, edges, band_sems, sems, done_sems = rest[-8:]
    chunks, _, block = window.shape
    k_count, double_rows, _ = pair_ref.shape
    rows = double_rows // 2
    band = core_ref.shape[-1]
    per_piece = chunks // pieces
    group = lax.axis_index("kgrp")
    state = lax.axis_index("orb") & 3
    starts = [0, HALO, HALO + rows, HALO + 2 * rows, HALO + 3 * rows]

    def columns_of(chunk):
        fixed, by_group, _ = places[chunk // per_piece]
        first = fixed + by_group * group + chunk % per_piece * block
        return pl.ds(pl.multiple_of(first, block), block)

    bands = [
        pltpu.make_async_copy(pair_source, pair_ref, band_sems.at[0]),
        pltpu.make_async_copy(core_ref, edges.at[1 - (state & 1)], band_sems.at[1]),
        pltpu.make_async_copy(chip_ref, edges.at[state & 1], band_sems.at[2]),
    ]
    for copy in bands:
        copy.start()
    for odd_chip in (0, 1):
        for odd_core in (0, 1):

            @pl.when(state == odd_chip * 2 + odd_core)
            def _():
                for chunk in range(chunks):
                    whole = columns_of(chunk)
                    index, place = chunk // per_piece, chunk % per_piece
                    piece = pl.ds(place * block, block)
                    sibling = sibling_ref.at[:, whole]
                    low = places[index][2]
                    near = near_chip_refs[index].at[0:rows, piece]
                    if odd_chip == odd_core:
                        near = near_onward_refs[index].at[low : low + rows, piece]
                    before, beyond = (chip_refs[index], 0), (onward_refs[index], low)
                    if odd_chip == 0:
                        before, beyond = beyond, before
                    (before, last), (beyond, first) = before, beyond
                    sources = [
                        before.at[last + rows - HALO : last + rows, piece],
                        sibling if odd_core else near,
                        own_ref.at[:, whole],
                        near if odd_core else sibling,
                        beyond.at[first : first + HALO, piece],
                    ]
                    for part, source in enumerate(sources):
                        count = source.shape[0]
                        target = window.at[chunk, starts[part] : starts[part] + count, :]
                        pltpu.make_async_copy(source, target, sems.at[chunk, part]).start()

    for copy in bands:
        copy.wait()

    def product(left, right):
        return jnp.dot(left, right, preferred_element_type=jnp.float32)

    own_band = jnp.concatenate([pair_ref[k][:, 0:band] for k in range(k_count)], axis=0)
    halo_rows = k_count * 2 * HALO

    def result_copy(chunk):
        return pltpu.make_async_copy(
            done.at[chunk], result_ref.at[:, :, :, columns_of(chunk)], done_sems.at[chunk]
        )

    for chunk in range(chunks):
        for part in range(5):
            count = HALO if part in (0, 4) else rows
            target = window.at[chunk, starts[part] : starts[part] + count, :]
            pltpu.make_async_copy(target, target, sems.at[chunk, part]).wait()
        lower = window[chunk, 0:band, :]
        middle = window[chunk, rows : rows + band, :]
        upper = window[chunk, 2 * rows : 2 * rows + band, :]
        own_first = product(own_band, middle).astype(jnp.bfloat16)
        left_first = product(edges[0].reshape(halo_rows, band), lower).astype(jnp.bfloat16)
        right_first = product(edges[1].reshape(halo_rows, band), upper).astype(jnp.bfloat16)
        center = window[chunk, HALO + rows : HALO + 2 * rows, :].astype(jnp.float32)
        for k in range(k_count):
            wide = jnp.concatenate(
                [
                    part
                    for kind in (2 * k, 2 * k + 1)
                    for part in (
                        left_first[kind * HALO : (kind + 1) * HALO],
                        own_first[kind * rows : (kind + 1) * rows],
                        right_first[kind * HALO : (kind + 1) * HALO],
                    )
                ],
                axis=0,
            )
            both = 2.0 * product(pair_ref[k], wide)
            done[chunk, k, 0] = (both[0:rows] - center).astype(jnp.bfloat16)
            done[chunk, k, 1] = both[rows:].astype(jnp.bfloat16)
        result_copy(chunk).start()
    for chunk in range(chunks):
        result_copy(chunk).wait()


def filter_columns(places, pair, core_band, chip_band, own, sibling, halos, so_far):
    k_count, double_rows, _ = pair.shape
    rows = double_rows // 2
    columns = own.shape[1]
    pieces = len(halos)
    width = halos[0][0].shape[1]
    block = min(BLOCK, width)
    chunks = pieces * width // block
    anywhere = pl.BlockSpec(memory_space=pl.ANY)
    hbm = pl.BlockSpec(memory_space=pltpu.HBM)
    operands = [pair, core_band, chip_band, own, sibling]
    operands += [halo[part] for part in range(4) for halo in halos]
    specs = [anywhere] * (5 + 4 * pieces)
    aliases = {}
    if so_far is not None:
        aliases = {len(operands): 0}
        operands.append(so_far)
        specs.append(hbm)
    return pl.pallas_call(
        functools.partial(filter_kernel, places),
        out_shape=jax.ShapeDtypeStruct((k_count, 2, rows, columns), jnp.bfloat16),
        in_specs=specs,
        out_specs=hbm,
        scratch_shapes=[
            pltpu.VMEM(pair.shape, jnp.bfloat16),
            pltpu.VMEM((chunks, 3 * rows + 2 * HALO, block), jnp.bfloat16),
            pltpu.VMEM((chunks, k_count, 2, rows, block), jnp.bfloat16),
            pltpu.VMEM((2,) + core_band.shape, jnp.bfloat16),
            pltpu.SemaphoreType.DMA((3,)),
            pltpu.SemaphoreType.DMA((chunks, 5)),
            pltpu.SemaphoreType.DMA((chunks,)),
        ],
        input_output_aliases=aliases,
        compiler_params=pltpu.CompilerParams(vmem_limit_bytes=40 << 20),
        cost_estimate=pl.CostEstimate(
            flops=0,
            bytes_accessed=0,
            transcendentals=0,
        ),
        name="filter_columns",
    )(*operands)


def local(hopping_tiles, tile_strip, tile_column_slot, lattice, kpoints, start_block):
    owners = lax.axis_size("orb")
    group = lax.axis_index("kgrp")
    step_count, tile_count, row_count, col_width = hopping_tiles.shape
    slot_count = (row_count + 2 * HALO) // col_width
    k_count = kpoints.shape[0]
    piece = start_block.shape[1] // 4

    dest = jnp.transpose(tile_strip, (1, 2, 0))
    tiles = hopping_tiles.reshape(step_count * tile_count, row_count, col_width)
    outgoing = pack_tiles(tiles, dest, owners)
    weights = receive_weights(kpoints, lattice.T, dest, tile_column_slot.T, owners, slot_count)
    incoming = lax.all_to_all(outgoing, "orb", split_axis=0, concat_axis=0, tiled=True)

    shared = to_pair_chip(lax.dynamic_slice_in_dim(start_block, group * piece, piece, axis=1))
    shared = after(shared, outgoing)
    third = to_pair_chip(after(start_block, shared)[:, 2 * piece : 3 * piece])
    near_shared = to_sibling(shared)
    sibling = to_sibling(start_block)
    shared_beyond = onward(shared)

    begun = begin_bands(weights, after(incoming, near_shared, sibling), k_count, slot_count)
    theirs = to_other_group(after(incoming, begun))
    third = after(third, begun)
    fourth = to_pair_chip(after(start_block, third, shared_beyond)[:, 3 * piece : 4 * piece])
    third_beyond = onward(third)
    pair, for_core, for_chip = make_bands(weights, theirs, begun, k_count, slot_count)
    core_band, chip_band = to_sibling(for_core), to_next_chip(for_chip)

    other = to_other_group(after(jnp.concatenate([shared, shared_beyond], axis=0), pair))
    fourth = after(fourth, core_band, chip_band)
    third_beyond = after(third_beyond, fourth)
    near_shared_beyond = to_sibling(after(shared_beyond, chip_band))
    near_third_beyond = to_sibling(third_beyond)
    near_third = to_sibling(after(third, pair))
    fourth_beyond = onward(fourth)
    near_fourth = to_sibling(fourth)

    def filtered(places, halos, so_far):
        return filter_columns(places, pair, core_band, chip_band, start_block, sibling, halos, so_far)

    result = filtered(
        [(0, piece, 0), (2 * piece, 0, 0)],
        [
            (shared, shared_beyond, near_shared, near_shared_beyond),
            (third, third_beyond, near_third, near_third_beyond),
        ],
        None,
    )
    other, fourth_beyond = after(other, result), after(fourth_beyond, result)
    near_other = to_sibling(other)
    return filtered(
        [(piece, -piece, row_count), (3 * piece, 0, 0)],
        [
            (other, other, near_other, near_other),
            (fourth, fourth_beyond, near_fourth, to_sibling(fourth_beyond)),
        ],
        result,
    )


def solution(mesh):
    return jax.shard_map(
        local,
        mesh=mesh,
        in_specs=(P("orb", None, None, None), P(), P(), P(), P("kgrp", None), P("orb", None)),
        out_specs=P("kgrp", None, "orb", None),
        check_vma=False,
    )
```

```python
import functools
import math

import jax
import jax.numpy as jnp
from jax import lax
from jax.experimental import pallas as pl
from jax.experimental.pallas import tpu as pltpu
from jax.sharding import PartitionSpec as P

HALO = 80
CAP = 2
LANES = 128
MUCH = 60 << 20
LITTLE = 32 << 20
BLOCK = 1024


def routed(value, route):
    groups, owners = lax.axis_size("kgrp"), lax.axis_size("orb")
    pairs = []
    for group in range(groups):
        for owner in range(owners):
            to_group, to_owner = route(group, owner)
            if 0 <= to_owner < owners:
                pairs.append((group * owners + owner, to_group * owners + to_owner))
    return lax.ppermute(value, ("kgrp", "orb"), pairs)


def to_sibling(value):
    return routed(value, lambda group, owner: (group, owner ^ 1))


def to_pair_chip(value):
    return routed(value, lambda group, owner: (group, owner ^ 2))


def onward(value):
    return routed(value, lambda group, owner: (group, owner + (4 if owner & 2 == 0 else -4)))


def to_other_group(value):
    return routed(value, lambda group, owner: (1 - group, owner))


def to_next_chip(value):
    return routed(value, lambda group, owner: (group, owner + (1 if owner & 1 else -1)))


def after(value, *sooner):
    return lax.optimization_barrier((value,) + sooner)[0]


def pack_kernel(dest_ref, tiles_ref, packed_ref, placed, source):
    slots = packed_ref.shape[0]
    tile_count = dest_ref.shape[0]
    step_count = tiles_ref.shape[0] // tile_count
    first_vector = lax.axis_index("orb") * step_count
    part = packed_ref.shape[1]
    rows = pl.ds(pl.multiple_of(lax.axis_index("kgrp") * part, part), part)

    def clear(slot, carry):
        source[slot] = 0
        return carry

    def forget(owner, carry):
        placed[owner] = 0
        return carry

    def place(tile, carry):
        dest = dest_ref[lax.rem(tile, tile_count), 0, first_vector + tile // tile_count]
        rank = placed[dest]
        placed[dest] = rank + 1
        source[dest * CAP + rank] = tile
        return carry

    def fill(slot, carry):
        packed_ref[slot] = tiles_ref[source[slot], rows, :]
        return carry

    lax.fori_loop(0, slots, clear, 0, unroll=4)
    lax.fori_loop(0, slots // CAP, forget, 0, unroll=4)
    lax.fori_loop(0, step_count * tile_count, place, 0)
    lax.fori_loop(0, slots, fill, 0, unroll=2)


def pack_tiles(tiles, dest, owners):
    slots = owners * CAP
    rows, width = tiles.shape[1:]
    vmem = pl.BlockSpec(memory_space=pltpu.VMEM)
    return pl.pallas_call(
        pack_kernel,
        out_shape=jax.ShapeDtypeStruct((slots, rows // lax.axis_size("kgrp"), width), tiles.dtype),
        in_specs=[pl.BlockSpec(memory_space=pltpu.SMEM), vmem],
        out_specs=vmem,
        scratch_shapes=[pltpu.SMEM((owners,), jnp.int32), pltpu.SMEM((slots,), jnp.int32)],
        compiler_params=pltpu.CompilerParams(vmem_limit_bytes=MUCH),
        cost_estimate=pl.CostEstimate(flops=0, bytes_accessed=0, transcendentals=0),
        name="pack_tiles",
    )(dest, tiles)


def weight_kernel(slot_count, *refs):
    sources, (weight_ref, point_ref, cell_ref, dest_ref, column_ref, sems) = refs[:4], refs[4:]
    copies = [
        pltpu.make_async_copy(source, target, sems.at[index])
        for index, (source, target) in enumerate(zip(sources, (point_ref, cell_ref, dest_ref, column_ref)))
    ]
    for copy in copies:
        copy.start()
    for copy in copies:
        copy.wait()
    tile_count, _, vectors = dest_ref.shape
    owners = weight_ref.shape[1] // LANES
    step_count = vectors // owners
    k_count = point_ref.shape[0]
    mine = dest_ref[:, 0, :] == lax.axis_index("orb")
    flags = mine.astype(jnp.float32)
    shape = (tile_count, tile_count)
    before = lax.broadcasted_iota(jnp.int32, shape, 1) < lax.broadcasted_iota(jnp.int32, shape, 0)
    rank = jnp.dot(before.astype(jnp.float32), flags, preferred_element_type=jnp.float32)
    shape = (vectors, vectors)
    sooner, later = lax.broadcasted_iota(jnp.int32, shape, 0), lax.broadcasted_iota(jnp.int32, shape, 1)
    same_owner = (sooner < later) & (sooner >= later - later % step_count)
    counts = jnp.broadcast_to(jnp.sum(flags, axis=0, keepdims=True), (8, vectors))
    above = jnp.dot(counts, same_owner.astype(jnp.float32), preferred_element_type=jnp.float32)
    rank = (rank + above[0:1]).astype(jnp.int32)
    cells = cell_ref[...].astype(jnp.float32)
    column = column_ref[...]
    values = []
    for k in range(k_count):
        fraction = point_ref[k, 0] * cells[0:1] + point_ref[k, 1] * cells[1:2]
        fraction = fraction + point_ref[k, 2] * cells[2:3]
        radians = 6.283185307179586 * fraction
        for wave in (jnp.cos(radians), jnp.sin(radians)):
            phase = wave.astype(jnp.bfloat16).astype(jnp.float32)
            for j in range(slot_count):
                for c in range(CAP):
                    here = mine & (rank == c) & (column == j)
                    values.append(jnp.sum(jnp.where(here, phase, 0.0), axis=0, keepdims=True))
    values = jnp.concatenate(values, axis=0)
    chunk = math.gcd(owners, 16)
    shape = (vectors, chunk * LANES)
    for first in range(0, owners, chunk):
        owner = first + lax.broadcasted_iota(jnp.int32, shape, 1) // LANES
        member = (lax.broadcasted_iota(jnp.int32, shape, 0) // step_count == owner).astype(jnp.float32)
        weight_ref[:, first * LANES : (first + chunk) * LANES] = jnp.dot(
            values, member, preferred_element_type=jnp.float32
        )


def receive_weights(kpoints, cells, dest, column, owners, slot_count):
    k_count = kpoints.shape[0]
    operands = (kpoints, cells, dest, column)
    spaces = (pltpu.SMEM, pltpu.VMEM, pltpu.VMEM, pltpu.VMEM)
    return pl.pallas_call(
        functools.partial(weight_kernel, slot_count),
        out_shape=jax.ShapeDtypeStruct((k_count * 2 * slot_count * CAP, owners * LANES), jnp.float32),
        in_specs=[pl.BlockSpec(memory_space=pltpu.HBM)] * 4,
        out_specs=pl.BlockSpec(memory_space=pltpu.VMEM),
        scratch_shapes=[space(array.shape, array.dtype) for space, array in zip(spaces, operands)]
        + [pltpu.SemaphoreType.DMA((4,))],
        compiler_params=pltpu.CompilerParams(vmem_limit_bytes=LITTLE),
        cost_estimate=pl.CostEstimate(flops=0, bytes_accessed=0, transcendentals=0),
        name="receive_weights",
    )(*operands)


def add_tiles(weight_ref, tiles_ref, pair_ref, index, k_count, slot_count):
    slots, part, width = tiles_ref.shape
    rows = pair_ref.shape[1] // 2
    band = slot_count * width
    kinds = k_count * 2 * slot_count

    def add(owner, totals):
        lanes = pl.ds(pl.multiple_of(owner * LANES, LANES), LANES)
        for c in range(CAP):
            tile = tiles_ref[owner * CAP + c].astype(jnp.float32)
            totals = tuple(
                total + weight_ref[pl.ds(kind * CAP + c, 1), lanes] * tile for kind, total in enumerate(totals)
            )
        return totals

    totals = lax.fori_loop(
        0, slots // CAP, add, tuple(jnp.zeros((part, width), jnp.float32) for _ in range(kinds))
    )
    top = pl.ds(pl.multiple_of(index * part, part), part)
    bottom = pl.ds(pl.multiple_of(rows + index * part, part), part)
    for k in range(k_count):
        for p in range(2):
            for j in range(slot_count):
                value = totals[(k * 2 + p) * slot_count + j].astype(jnp.bfloat16)
                columns = slice(j * width, (j + 1) * width)
                later = slice(band + j * width, band + (j + 1) * width)
                if p == 0:
                    pair_ref[k, top, columns] = value
                    pair_ref[k, bottom, later] = value
                else:
                    pair_ref[k, bottom, columns] = value
                    pair_ref[k, top, later] = -value


def begin_kernel(k_count, slot_count, weight_ref, tiles_ref, pair_ref):
    add_tiles(weight_ref, tiles_ref, pair_ref, lax.axis_index("kgrp"), k_count, slot_count)


def band_kernel(k_count, slot_count, weight_ref, tiles_ref, begun_ref, pair_ref, core_ref, chip_ref):
    rows = pair_ref.shape[1] // 2
    band = core_ref.shape[-1]
    pair_ref[...] = begun_ref[...]
    add_tiles(weight_ref, tiles_ref, pair_ref, 1 - lax.axis_index("kgrp"), k_count, slot_count)
    odd_core = lax.axis_index("orb") & 1
    for odd in (0, 1):

        @pl.when(odd_core == odd)
        def _():
            tail_ref, head_ref = (chip_ref, core_ref) if odd else (core_ref, chip_ref)
            for k in range(k_count):
                for p in range(2):
                    tail_ref[k, p] = pair_ref[k, (p + 1) * rows - HALO : (p + 1) * rows, 0:band]
                    head_ref[k, p] = pair_ref[k, p * rows : p * rows + HALO, 0:band]


def begin_bands(weights, tiles, k_count, slot_count):
    part, width = tiles.shape[1:]
    vmem = pl.BlockSpec(memory_space=pltpu.VMEM)
    return pl.pallas_call(
        functools.partial(begin_kernel, k_count, slot_count),
        out_shape=jax.ShapeDtypeStruct((k_count, 4 * part, 2 * slot_count * width), jnp.bfloat16),
        in_specs=[vmem, vmem],
        out_specs=vmem,
        compiler_params=pltpu.CompilerParams(vmem_limit_bytes=LITTLE),
        cost_estimate=pl.CostEstimate(flops=0, bytes_accessed=0, transcendentals=0),
        name="begin_bands",
    )(weights, tiles)


def make_bands(weights, tiles, begun, k_count, slot_count):
    band = slot_count * tiles.shape[2]
    edge = (k_count, 2, HALO, band)
    vmem = pl.BlockSpec(memory_space=pltpu.VMEM)
    return pl.pallas_call(
        functools.partial(band_kernel, k_count, slot_count),
        out_shape=[jax.ShapeDtypeStruct(shape, jnp.bfloat16) for shape in (begun.shape, edge, edge)],
        in_specs=[vmem, vmem, vmem],
        out_specs=[vmem, vmem, vmem],
        compiler_params=pltpu.CompilerParams(vmem_limit_bytes=LITTLE),
        cost_estimate=pl.CostEstimate(flops=0, bytes_accessed=0, transcendentals=0),
        name="make_bands",
    )(weights, tiles, begun)


def filter_kernel(places, pair_source, core_ref, chip_ref, own_ref, sibling_ref, *rest):
    pieces = len(places)
    chip_refs, onward_refs, near_chip_refs, near_onward_refs = (
        rest[part * pieces : (part + 1) * pieces] for part in range(4)
    )
    result_ref, pair_ref, window, done, edges, band_sems, sems, done_sems = rest[-8:]
    chunks, _, block = window.shape
    k_count, double_rows, _ = pair_ref.shape
    rows = double_rows // 2
    band = core_ref.shape[-1]
    per_piece = chunks // pieces
    group = lax.axis_index("kgrp")
    state = lax.axis_index("orb") & 3
    starts = [0, HALO, HALO + rows, HALO + 2 * rows, HALO + 3 * rows]

    def columns_of(chunk):
        fixed, by_group, _ = places[chunk // per_piece]
        first = fixed + by_group * group + chunk % per_piece * block
        return pl.ds(pl.multiple_of(first, block), block)

    bands = [
        pltpu.make_async_copy(pair_source, pair_ref, band_sems.at[0]),
        pltpu.make_async_copy(core_ref, edges.at[1 - (state & 1)], band_sems.at[1]),
        pltpu.make_async_copy(chip_ref, edges.at[state & 1], band_sems.at[2]),
    ]
    for copy in bands:
        copy.start()
    for odd_chip in (0, 1):
        for odd_core in (0, 1):

            @pl.when(state == odd_chip * 2 + odd_core)
            def _():
                for chunk in range(chunks):
                    whole = columns_of(chunk)
                    index, place = chunk // per_piece, chunk % per_piece
                    piece = pl.ds(place * block, block)
                    sibling = sibling_ref.at[:, whole]
                    low = places[index][2]
                    near = near_chip_refs[index].at[0:rows, piece]
                    if odd_chip == odd_core:
                        near = near_onward_refs[index].at[low : low + rows, piece]
                    before, beyond = (chip_refs[index], 0), (onward_refs[index], low)
                    if odd_chip == 0:
                        before, beyond = beyond, before
                    (before, last), (beyond, first) = before, beyond
                    sources = [
                        before.at[last + rows - HALO : last + rows, piece],
                        sibling if odd_core else near,
                        own_ref.at[:, whole],
                        near if odd_core else sibling,
                        beyond.at[first : first + HALO, piece],
                    ]
                    for part, source in enumerate(sources):
                        count = source.shape[0]
                        target = window.at[chunk, starts[part] : starts[part] + count, :]
                        pltpu.make_async_copy(source, target, sems.at[chunk, part]).start()

    for copy in bands:
        copy.wait()

    def product(left, right):
        return jnp.dot(left, right, preferred_element_type=jnp.float32)

    own_band = jnp.concatenate([pair_ref[k][:, 0:band] for k in range(k_count)], axis=0)
    halo_rows = k_count * 2 * HALO

    def result_copy(chunk):
        return pltpu.make_async_copy(
            done.at[chunk], result_ref.at[:, :, :, columns_of(chunk)], done_sems.at[chunk]
        )

    for chunk in range(chunks):
        for part in range(5):
            count = HALO if part in (0, 4) else rows
            target = window.at[chunk, starts[part] : starts[part] + count, :]
            pltpu.make_async_copy(target, target, sems.at[chunk, part]).wait()
        lower = window[chunk, 0:band, :]
        middle = window[chunk, rows : rows + band, :]
        upper = window[chunk, 2 * rows : 2 * rows + band, :]
        own_first = product(own_band, middle).astype(jnp.bfloat16)
        left_first = product(edges[0].reshape(halo_rows, band), lower).astype(jnp.bfloat16)
        right_first = product(edges[1].reshape(halo_rows, band), upper).astype(jnp.bfloat16)
        center = window[chunk, HALO + rows : HALO + 2 * rows, :].astype(jnp.float32)
        for k in range(k_count):
            wide = jnp.concatenate(
                [
                    part
                    for kind in (2 * k, 2 * k + 1)
                    for part in (
                        left_first[kind * HALO : (kind + 1) * HALO],
                        own_first[kind * rows : (kind + 1) * rows],
                        right_first[kind * HALO : (kind + 1) * HALO],
                    )
                ],
                axis=0,
            )
            both = 2.0 * product(pair_ref[k], wide)
            done[chunk, k, 0] = (both[0:rows] - center).astype(jnp.bfloat16)
            done[chunk, k, 1] = both[rows:].astype(jnp.bfloat16)
        result_copy(chunk).start()
    for chunk in range(chunks):
        result_copy(chunk).wait()


def filter_columns(places, pair, core_band, chip_band, own, sibling, halos, so_far):
    k_count, double_rows, _ = pair.shape
    rows = double_rows // 2
    columns = own.shape[1]
    pieces = len(halos)
    width = halos[0][0].shape[1]
    block = min(BLOCK, width)
    chunks = pieces * width // block
    anywhere = pl.BlockSpec(memory_space=pl.ANY)
    hbm = pl.BlockSpec(memory_space=pltpu.HBM)
    operands = [pair, core_band, chip_band, own, sibling]
    operands += [halo[part] for part in range(4) for halo in halos]
    specs = [anywhere] * (5 + 4 * pieces)
    aliases = {}
    if so_far is not None:
        aliases = {len(operands): 0}
        operands.append(so_far)
        specs.append(hbm)
    return pl.pallas_call(
        functools.partial(filter_kernel, places),
        out_shape=jax.ShapeDtypeStruct((k_count, 2, rows, columns), jnp.bfloat16),
        in_specs=specs,
        out_specs=hbm,
        scratch_shapes=[
            pltpu.VMEM(pair.shape, jnp.bfloat16),
            pltpu.VMEM((chunks, 3 * rows + 2 * HALO, block), jnp.bfloat16),
            pltpu.VMEM((chunks, k_count, 2, rows, block), jnp.bfloat16),
            pltpu.VMEM((2,) + core_band.shape, jnp.bfloat16),
            pltpu.SemaphoreType.DMA((3,)),
            pltpu.SemaphoreType.DMA((chunks, 5)),
            pltpu.SemaphoreType.DMA((chunks,)),
        ],
        input_output_aliases=aliases,
        compiler_params=pltpu.CompilerParams(vmem_limit_bytes=49 << 20),
        cost_estimate=pl.CostEstimate(
            flops=0,
            bytes_accessed=0,
            transcendentals=0,
        ),
        name="filter_columns",
    )(*operands)


def local(hopping_tiles, tile_strip, tile_column_slot, lattice, kpoints, start_block):
    owners = lax.axis_size("orb")
    group = lax.axis_index("kgrp")
    step_count, tile_count, row_count, col_width = hopping_tiles.shape
    slot_count = (row_count + 2 * HALO) // col_width
    k_count = kpoints.shape[0]
    piece = start_block.shape[1] // 4

    dest = jnp.transpose(tile_strip, (1, 2, 0))
    tiles = hopping_tiles.reshape(step_count * tile_count, row_count, col_width)
    outgoing = pack_tiles(tiles, dest, owners)
    weights = receive_weights(kpoints, lattice.T, dest, tile_column_slot.T, owners, slot_count)
    incoming = lax.all_to_all(outgoing, "orb", split_axis=0, concat_axis=0, tiled=True)

    shared = to_pair_chip(lax.dynamic_slice_in_dim(start_block, group * piece, piece, axis=1))
    shared = after(shared, outgoing)
    third = to_pair_chip(after(start_block, shared)[:, 2 * piece : 3 * piece])
    near_shared = to_sibling(shared)
    sibling = to_sibling(start_block)
    shared_beyond = onward(shared)

    last = after(start_block, shared)[:, 3 * piece : 4 * piece]
    begun = begin_bands(weights, after(incoming, near_shared, sibling, last), k_count, slot_count)
    theirs = to_other_group(after(incoming, begun))
    third = after(third, begun)
    fourth = to_pair_chip(after(last, third, shared_beyond))
    third_beyond = onward(third)
    pair, for_core, for_chip = make_bands(weights, theirs, begun, k_count, slot_count)
    core_band, chip_band = to_sibling(for_core), to_next_chip(for_chip)

    other = to_other_group(after(jnp.concatenate([shared, shared_beyond], axis=0), pair))
    fourth = after(fourth, core_band, chip_band)
    third_beyond = after(third_beyond, fourth)
    near_shared_beyond = to_sibling(after(shared_beyond, chip_band))
    near_third_beyond = to_sibling(third_beyond)
    near_third = to_sibling(after(third, pair))
    fourth_beyond = onward(fourth)
    near_fourth = to_sibling(fourth)

    def filtered(places, halos, so_far):
        return filter_columns(places, pair, core_band, chip_band, start_block, sibling, halos, so_far)

    result = filtered(
        [(0, piece, 0), (2 * piece, 0, 0)],
        [
            (shared, shared_beyond, near_shared, near_shared_beyond),
            (third, third_beyond, near_third, near_third_beyond),
        ],
        None,
    )
    other, fourth_beyond = after(other, result), after(fourth_beyond, result)
    near_other = to_sibling(other)
    return filtered(
        [(piece, -piece, row_count), (3 * piece, 0, 0)],
        [
            (other, other, near_other, near_other),
            (fourth, fourth_beyond, near_fourth, to_sibling(fourth_beyond)),
        ],
        result,
    )


def solution(mesh):
    return jax.shard_map(
        local,
        mesh=mesh,
        in_specs=(P("orb", None, None, None), P(), P(), P(), P("kgrp", None), P("orb", None)),
        out_specs=P("kgrp", None, "orb", None),
        check_vma=False,
    )
```

```python
import functools
import math

import jax
import jax.numpy as jnp
from jax import lax
from jax.experimental import pallas as pl
from jax.experimental.pallas import tpu as pltpu
from jax.sharding import PartitionSpec as P

HALO = 80
CAP = 2
LANES = 128
MUCH = 60 << 20
LITTLE = 32 << 20
BLOCK = 1024


def routed(value, route):
    groups, owners = lax.axis_size("kgrp"), lax.axis_size("orb")
    pairs = []
    for group in range(groups):
        for owner in range(owners):
            to_group, to_owner = route(group, owner)
            if 0 <= to_owner < owners:
                pairs.append((group * owners + owner, to_group * owners + to_owner))
    return lax.ppermute(value, ("kgrp", "orb"), pairs)


def to_sibling(value):
    return routed(value, lambda group, owner: (group, owner ^ 1))


def to_pair_chip(value):
    return routed(value, lambda group, owner: (group, owner ^ 2))


def onward(value):
    return routed(value, lambda group, owner: (group, owner + (4 if owner & 2 == 0 else -4)))


def to_other_group(value):
    return routed(value, lambda group, owner: (1 - group, owner))


def to_next_chip(value):
    return routed(value, lambda group, owner: (group, owner + (1 if owner & 1 else -1)))


def after(value, *sooner):
    return lax.optimization_barrier((value,) + sooner)[0]


def pack_kernel(dest_ref, tiles_ref, packed_ref, placed, source, held, arrived):
    slots, part, _ = packed_ref.shape
    tile_count = dest_ref.shape[0]
    step_count = tiles_ref.shape[0] // tile_count
    first_vector = lax.axis_index("orb") * step_count
    rows = pl.ds(pl.multiple_of(lax.axis_index("kgrp") * part, part), part)
    fetch = pltpu.make_async_copy(tiles_ref.at[:, rows, :], held, arrived)
    fetch.start()

    def clear(slot, carry):
        source[slot] = 0
        return carry

    def forget(owner, carry):
        placed[owner] = 0
        return carry

    def place(tile, carry):
        dest = dest_ref[lax.rem(tile, tile_count), 0, first_vector + tile // tile_count]
        rank = placed[dest]
        placed[dest] = rank + 1
        source[dest * CAP + rank] = tile
        return carry

    lax.fori_loop(0, slots, clear, 0, unroll=4)
    lax.fori_loop(0, slots // CAP, forget, 0, unroll=4)
    lax.fori_loop(0, step_count * tile_count, place, 0)
    fetch.wait()

    def fill(slot, carry):
        packed_ref[slot] = held[source[slot]]
        return carry

    lax.fori_loop(0, slots, fill, 0, unroll=4)


def pack_tiles(tiles, dest, owners):
    slots = owners * CAP
    tile_total, rows, width = tiles.shape
    part = rows // lax.axis_size("kgrp")
    return pl.pallas_call(
        pack_kernel,
        out_shape=jax.ShapeDtypeStruct((slots, part, width), tiles.dtype),
        in_specs=[pl.BlockSpec(memory_space=pltpu.SMEM), pl.BlockSpec(memory_space=pltpu.HBM)],
        out_specs=pl.BlockSpec(memory_space=pltpu.VMEM),
        scratch_shapes=[
            pltpu.SMEM((owners,), jnp.int32),
            pltpu.SMEM((slots,), jnp.int32),
            pltpu.VMEM((tile_total, part, width), tiles.dtype),
            pltpu.SemaphoreType.DMA,
        ],
        compiler_params=pltpu.CompilerParams(vmem_limit_bytes=MUCH),
        cost_estimate=pl.CostEstimate(flops=0, bytes_accessed=0, transcendentals=0),
        name="pack_tiles",
    )(dest, tiles)


def weight_kernel(slot_count, *refs):
    sources, (weight_ref, point_ref, cell_ref, dest_ref, column_ref, sems) = refs[:4], refs[4:]
    copies = [
        pltpu.make_async_copy(source, target, sems.at[index])
        for index, (source, target) in enumerate(zip(sources, (point_ref, cell_ref, dest_ref, column_ref)))
    ]
    for copy in copies:
        copy.start()
    for copy in copies:
        copy.wait()
    tile_count, _, vectors = dest_ref.shape
    owners = weight_ref.shape[1] // LANES
    step_count = vectors // owners
    k_count = point_ref.shape[0]
    mine = dest_ref[:, 0, :] == lax.axis_index("orb")
    flags = mine.astype(jnp.float32)
    shape = (tile_count, tile_count)
    before = lax.broadcasted_iota(jnp.int32, shape, 1) < lax.broadcasted_iota(jnp.int32, shape, 0)
    rank = jnp.dot(before.astype(jnp.float32), flags, preferred_element_type=jnp.float32)
    shape = (vectors, vectors)
    sooner, later = lax.broadcasted_iota(jnp.int32, shape, 0), lax.broadcasted_iota(jnp.int32, shape, 1)
    same_owner = (sooner < later) & (sooner >= later - later % step_count)
    counts = jnp.broadcast_to(jnp.sum(flags, axis=0, keepdims=True), (8, vectors))
    above = jnp.dot(counts, same_owner.astype(jnp.float32), preferred_element_type=jnp.float32)
    rank = (rank + above[0:1]).astype(jnp.int32)
    cells = cell_ref[...].astype(jnp.float32)
    column = column_ref[...]
    values = []
    for k in range(k_count):
        fraction = point_ref[k, 0] * cells[0:1] + point_ref[k, 1] * cells[1:2]
        fraction = fraction + point_ref[k, 2] * cells[2:3]
        radians = 6.283185307179586 * fraction
        for wave in (jnp.cos(radians), jnp.sin(radians)):
            phase = wave.astype(jnp.bfloat16).astype(jnp.float32)
            for j in range(slot_count):
                for c in range(CAP):
                    here = mine & (rank == c) & (column == j)
                    values.append(jnp.sum(jnp.where(here, phase, 0.0), axis=0, keepdims=True))
    values = jnp.concatenate(values, axis=0)
    chunk = math.gcd(owners, 16)
    shape = (vectors, chunk * LANES)
    for first in range(0, owners, chunk):
        owner = first + lax.broadcasted_iota(jnp.int32, shape, 1) // LANES
        member = (lax.broadcasted_iota(jnp.int32, shape, 0) // step_count == owner).astype(jnp.float32)
        weight_ref[:, first * LANES : (first + chunk) * LANES] = jnp.dot(
            values, member, preferred_element_type=jnp.float32
        )


def receive_weights(kpoints, cells, dest, column, owners, slot_count):
    k_count = kpoints.shape[0]
    operands = (kpoints, cells, dest, column)
    spaces = (pltpu.SMEM, pltpu.VMEM, pltpu.VMEM, pltpu.VMEM)
    return pl.pallas_call(
        functools.partial(weight_kernel, slot_count),
        out_shape=jax.ShapeDtypeStruct((k_count * 2 * slot_count * CAP, owners * LANES), jnp.float32),
        in_specs=[pl.BlockSpec(memory_space=pltpu.HBM)] * 4,
        out_specs=pl.BlockSpec(memory_space=pltpu.VMEM),
        scratch_shapes=[space(array.shape, array.dtype) for space, array in zip(spaces, operands)]
        + [pltpu.SemaphoreType.DMA((4,))],
        compiler_params=pltpu.CompilerParams(vmem_limit_bytes=LITTLE),
        cost_estimate=pl.CostEstimate(flops=0, bytes_accessed=0, transcendentals=0),
        name="receive_weights",
    )(*operands)


def add_tiles(weight_ref, tiles_ref, pair_ref, index, k_count, slot_count):
    slots, part, width = tiles_ref.shape
    rows = pair_ref.shape[1] // 2
    band = slot_count * width
    kinds = k_count * 2 * slot_count

    def add(owner, totals):
        lanes = pl.ds(pl.multiple_of(owner * LANES, LANES), LANES)
        for c in range(CAP):
            tile = tiles_ref[owner * CAP + c].astype(jnp.float32)
            totals = tuple(
                total + weight_ref[pl.ds(kind * CAP + c, 1), lanes] * tile for kind, total in enumerate(totals)
            )
        return totals

    totals = lax.fori_loop(
        0, slots // CAP, add, tuple(jnp.zeros((part, width), jnp.float32) for _ in range(kinds))
    )
    top = pl.ds(pl.multiple_of(index * part, part), part)
    bottom = pl.ds(pl.multiple_of(rows + index * part, part), part)
    for k in range(k_count):
        for p in range(2):
            for j in range(slot_count):
                value = totals[(k * 2 + p) * slot_count + j].astype(jnp.bfloat16)
                columns = slice(j * width, (j + 1) * width)
                later = slice(band + j * width, band + (j + 1) * width)
                if p == 0:
                    pair_ref[k, top, columns] = value
                    pair_ref[k, bottom, later] = value
                else:
                    pair_ref[k, bottom, columns] = value
                    pair_ref[k, top, later] = -value


def begin_kernel(k_count, slot_count, weight_ref, tiles_ref, pair_ref):
    add_tiles(weight_ref, tiles_ref, pair_ref, lax.axis_index("kgrp"), k_count, slot_count)


def band_kernel(k_count, slot_count, weight_ref, tiles_ref, begun_ref, pair_ref, core_ref, chip_ref):
    rows = pair_ref.shape[1] // 2
    band = core_ref.shape[-1]
    pair_ref[...] = begun_ref[...]
    add_tiles(weight_ref, tiles_ref, pair_ref, 1 - lax.axis_index("kgrp"), k_count, slot_count)
    odd_core = lax.axis_index("orb") & 1
    for odd in (0, 1):

        @pl.when(odd_core == odd)
        def _():
            tail_ref, head_ref = (chip_ref, core_ref) if odd else (core_ref, chip_ref)
            for k in range(k_count):
                for p in range(2):
                    tail_ref[k, p] = pair_ref[k, (p + 1) * rows - HALO : (p + 1) * rows, 0:band]
                    head_ref[k, p] = pair_ref[k, p * rows : p * rows + HALO, 0:band]


def begin_bands(weights, tiles, k_count, slot_count):
    part, width = tiles.shape[1:]
    vmem = pl.BlockSpec(memory_space=pltpu.VMEM)
    return pl.pallas_call(
        functools.partial(begin_kernel, k_count, slot_count),
        out_shape=jax.ShapeDtypeStruct((k_count, 4 * part, 2 * slot_count * width), jnp.bfloat16),
        in_specs=[vmem, vmem],
        out_specs=vmem,
        compiler_params=pltpu.CompilerParams(vmem_limit_bytes=LITTLE),
        cost_estimate=pl.CostEstimate(flops=0, bytes_accessed=0, transcendentals=0),
        name="begin_bands",
    )(weights, tiles)


def make_bands(weights, tiles, begun, k_count, slot_count):
    band = slot_count * tiles.shape[2]
    edge = (k_count, 2, HALO, band)
    vmem = pl.BlockSpec(memory_space=pltpu.VMEM)
    return pl.pallas_call(
        functools.partial(band_kernel, k_count, slot_count),
        out_shape=[jax.ShapeDtypeStruct(shape, jnp.bfloat16) for shape in (begun.shape, edge, edge)],
        in_specs=[vmem, vmem, vmem],
        out_specs=[vmem, vmem, vmem],
        compiler_params=pltpu.CompilerParams(vmem_limit_bytes=LITTLE),
        cost_estimate=pl.CostEstimate(flops=0, bytes_accessed=0, transcendentals=0),
        name="make_bands",
    )(weights, tiles, begun)


def filter_kernel(places, pair_source, core_ref, chip_ref, own_ref, sibling_ref, *rest):
    pieces = len(places)
    chip_refs, onward_refs, near_chip_refs, near_onward_refs = (
        rest[part * pieces : (part + 1) * pieces] for part in range(4)
    )
    result_ref, pair_ref, window, done, edges, band_sems, sems, done_sems = rest[-8:]
    chunks, _, block = window.shape
    k_count, double_rows, _ = pair_ref.shape
    rows = double_rows // 2
    band = core_ref.shape[-1]
    per_piece = chunks // pieces
    group = lax.axis_index("kgrp")
    state = lax.axis_index("orb") & 3
    starts = [0, HALO, HALO + rows, HALO + 2 * rows, HALO + 3 * rows]

    def columns_of(chunk):
        fixed, by_group, _ = places[chunk // per_piece]
        first = fixed + by_group * group + chunk % per_piece * block
        return pl.ds(pl.multiple_of(first, block), block)

    bands = [
        pltpu.make_async_copy(pair_source, pair_ref, band_sems.at[0]),
        pltpu.make_async_copy(core_ref, edges.at[1 - (state & 1)], band_sems.at[1]),
        pltpu.make_async_copy(chip_ref, edges.at[state & 1], band_sems.at[2]),
    ]
    for copy in bands:
        copy.start()
    for odd_chip in (0, 1):
        for odd_core in (0, 1):

            @pl.when(state == odd_chip * 2 + odd_core)
            def _():
                for chunk in range(chunks):
                    whole = columns_of(chunk)
                    index, place = chunk // per_piece, chunk % per_piece
                    piece = pl.ds(place * block, block)
                    sibling = sibling_ref.at[:, whole]
                    low = places[index][2]
                    near = near_chip_refs[index].at[0:rows, piece]
                    if odd_chip == odd_core:
                        near = near_onward_refs[index].at[low : low + rows, piece]
                    before, beyond = (chip_refs[index], 0), (onward_refs[index], low)
                    if odd_chip == 0:
                        before, beyond = beyond, before
                    (before, last), (beyond, first) = before, beyond
                    sources = [
                        before.at[last + rows - HALO : last + rows, piece],
                        sibling if odd_core else near,
                        own_ref.at[:, whole],
                        near if odd_core else sibling,
                        beyond.at[first : first + HALO, piece],
                    ]
                    for part, source in enumerate(sources):
                        count = source.shape[0]
                        target = window.at[chunk, starts[part] : starts[part] + count, :]
                        pltpu.make_async_copy(source, target, sems.at[chunk, part]).start()

    for copy in bands:
        copy.wait()

    def product(left, right):
        return jnp.dot(left, right, preferred_element_type=jnp.float32)

    own_band = jnp.concatenate([pair_ref[k][:, 0:band] for k in range(k_count)], axis=0)
    halo_rows = k_count * 2 * HALO

    def result_copy(chunk):
        return pltpu.make_async_copy(
            done.at[chunk], result_ref.at[:, :, :, columns_of(chunk)], done_sems.at[chunk]
        )

    for chunk in range(chunks):
        for part in range(5):
            count = HALO if part in (0, 4) else rows
            target = window.at[chunk, starts[part] : starts[part] + count, :]
            pltpu.make_async_copy(target, target, sems.at[chunk, part]).wait()
        lower = window[chunk, 0:band, :]
        middle = window[chunk, rows : rows + band, :]
        upper = window[chunk, 2 * rows : 2 * rows + band, :]
        own_first = product(own_band, middle).astype(jnp.bfloat16)
        left_first = product(edges[0].reshape(halo_rows, band), lower).astype(jnp.bfloat16)
        right_first = product(edges[1].reshape(halo_rows, band), upper).astype(jnp.bfloat16)
        center = window[chunk, HALO + rows : HALO + 2 * rows, :].astype(jnp.float32)
        for k in range(k_count):
            wide = jnp.concatenate(
                [
                    part
                    for kind in (2 * k, 2 * k + 1)
                    for part in (
                        left_first[kind * HALO : (kind + 1) * HALO],
                        own_first[kind * rows : (kind + 1) * rows],
                        right_first[kind * HALO : (kind + 1) * HALO],
                    )
                ],
                axis=0,
            )
            both = 2.0 * product(pair_ref[k], wide)
            done[chunk, k, 0] = (both[0:rows] - center).astype(jnp.bfloat16)
            done[chunk, k, 1] = both[rows:].astype(jnp.bfloat16)
        result_copy(chunk).start()
    for chunk in range(chunks):
        result_copy(chunk).wait()


def filter_columns(places, pair, core_band, chip_band, own, sibling, halos, so_far):
    k_count, double_rows, _ = pair.shape
    rows = double_rows // 2
    columns = own.shape[1]
    pieces = len(halos)
    width = halos[0][0].shape[1]
    block = min(BLOCK, width)
    chunks = pieces * width // block
    anywhere = pl.BlockSpec(memory_space=pl.ANY)
    hbm = pl.BlockSpec(memory_space=pltpu.HBM)
    operands = [pair, core_band, chip_band, own, sibling]
    operands += [halo[part] for part in range(4) for halo in halos]
    specs = [anywhere] * (5 + 4 * pieces)
    aliases = {}
    if so_far is not None:
        aliases = {len(operands): 0}
        operands.append(so_far)
        specs.append(hbm)
    return pl.pallas_call(
        functools.partial(filter_kernel, places),
        out_shape=jax.ShapeDtypeStruct((k_count, 2, rows, columns), jnp.bfloat16),
        in_specs=specs,
        out_specs=hbm,
        scratch_shapes=[
            pltpu.VMEM(pair.shape, jnp.bfloat16),
            pltpu.VMEM((chunks, 3 * rows + 2 * HALO, block), jnp.bfloat16),
            pltpu.VMEM((chunks, k_count, 2, rows, block), jnp.bfloat16),
            pltpu.VMEM((2,) + core_band.shape, jnp.bfloat16),
            pltpu.SemaphoreType.DMA((3,)),
            pltpu.SemaphoreType.DMA((chunks, 5)),
            pltpu.SemaphoreType.DMA((chunks,)),
        ],
        input_output_aliases=aliases,
        compiler_params=pltpu.CompilerParams(vmem_limit_bytes=49 << 20),
        cost_estimate=pl.CostEstimate(
            flops=0,
            bytes_accessed=0,
            transcendentals=0,
        ),
        name="filter_columns",
    )(*operands)


def local(hopping_tiles, tile_strip, tile_column_slot, lattice, kpoints, start_block):
    owners = lax.axis_size("orb")
    group = lax.axis_index("kgrp")
    step_count, tile_count, row_count, col_width = hopping_tiles.shape
    slot_count = (row_count + 2 * HALO) // col_width
    k_count = kpoints.shape[0]
    piece = start_block.shape[1] // 4

    dest = jnp.transpose(tile_strip, (1, 2, 0))
    tiles = hopping_tiles.reshape(step_count * tile_count, row_count, col_width)
    outgoing = pack_tiles(tiles, dest, owners)
    weights = receive_weights(kpoints, lattice.T, dest, tile_column_slot.T, owners, slot_count)
    incoming = lax.all_to_all(outgoing, "orb", split_axis=0, concat_axis=0, tiled=True)

    shared = to_pair_chip(lax.dynamic_slice_in_dim(start_block, group * piece, piece, axis=1))
    shared = after(shared, outgoing)
    third = to_pair_chip(after(start_block, shared)[:, 2 * piece : 3 * piece])
    near_shared = to_sibling(shared)
    sibling = to_sibling(start_block)
    shared_beyond = onward(shared)

    last = after(start_block, shared)[:, 3 * piece : 4 * piece]
    begun = begin_bands(weights, after(incoming, near_shared, sibling, last), k_count, slot_count)
    theirs = to_other_group(after(incoming, begun))
    third = after(third, begun)
    fourth = to_pair_chip(after(last, third, shared_beyond))
    third_beyond = onward(third)
    pair, for_core, for_chip = make_bands(weights, theirs, begun, k_count, slot_count)
    core_band, chip_band = to_sibling(for_core), to_next_chip(for_chip)

    other = to_other_group(after(jnp.concatenate([shared, shared_beyond], axis=0), pair))
    fourth = after(fourth, core_band, chip_band)
    third_beyond = after(third_beyond, fourth)
    near_shared_beyond = to_sibling(after(shared_beyond, chip_band))
    near_third_beyond = to_sibling(third_beyond)
    near_third = to_sibling(after(third, pair))
    fourth_beyond = onward(fourth)
    near_fourth = to_sibling(fourth)

    def filtered(places, halos, so_far):
        return filter_columns(places, pair, core_band, chip_band, start_block, sibling, halos, so_far)

    result = filtered(
        [(0, piece, 0), (2 * piece, 0, 0)],
        [
            (shared, shared_beyond, near_shared, near_shared_beyond),
            (third, third_beyond, near_third, near_third_beyond),
        ],
        None,
    )
    other, fourth_beyond = after(other, result), after(fourth_beyond, result)
    near_other = to_sibling(other)
    return filtered(
        [(piece, -piece, row_count), (3 * piece, 0, 0)],
        [
            (other, other, near_other, near_other),
            (fourth, fourth_beyond, near_fourth, to_sibling(fourth_beyond)),
        ],
        result,
    )


def solution(mesh):
    return jax.shard_map(
        local,
        mesh=mesh,
        in_specs=(P("orb", None, None, None), P(), P(), P(), P("kgrp", None), P("orb", None)),
        out_specs=P("kgrp", None, "orb", None),
        check_vma=False,
    )
```

```python
import functools
import math

import jax
import jax.numpy as jnp
from jax import lax
from jax.experimental import pallas as pl
from jax.experimental.pallas import tpu as pltpu
from jax.sharding import PartitionSpec as P

HALO = 80
CAP = 2
LANES = 128
MUCH = 60 << 20
LITTLE = 32 << 20
BLOCK = 1024


def routed(value, route):
    groups, owners = lax.axis_size("kgrp"), lax.axis_size("orb")
    pairs = []
    for group in range(groups):
        for owner in range(owners):
            to_group, to_owner = route(group, owner)
            if 0 <= to_owner < owners:
                pairs.append((group * owners + owner, to_group * owners + to_owner))
    return lax.ppermute(value, ("kgrp", "orb"), pairs)


def to_sibling(value):
    return routed(value, lambda group, owner: (group, owner ^ 1))


def to_pair_chip(value):
    return routed(value, lambda group, owner: (group, owner ^ 2))


def onward(value):
    return routed(value, lambda group, owner: (group, owner + (4 if owner & 2 == 0 else -4)))


def to_other_group(value):
    return routed(value, lambda group, owner: (1 - group, owner))


def to_next_chip(value):
    return routed(value, lambda group, owner: (group, owner + (1 if owner & 1 else -1)))


def after(value, *sooner):
    return lax.optimization_barrier((value,) + sooner)[0]


def pack_kernel(dest_ref, tiles_ref, packed_ref, placed, source):
    slots = packed_ref.shape[0]
    tile_count = dest_ref.shape[0]
    step_count = tiles_ref.shape[0] // tile_count
    first_vector = lax.axis_index("orb") * step_count
    part = packed_ref.shape[1]
    rows = pl.ds(pl.multiple_of(lax.axis_index("kgrp") * part, part), part)

    def clear(slot, carry):
        source[slot] = 0
        return carry

    def forget(owner, carry):
        placed[owner] = 0
        return carry

    def place(tile, carry):
        dest = dest_ref[lax.rem(tile, tile_count), 0, first_vector + tile // tile_count]
        rank = placed[dest]
        placed[dest] = rank + 1
        source[dest * CAP + rank] = tile
        return carry

    def fill(slot, carry):
        packed_ref[slot] = tiles_ref[source[slot], rows, :]
        return carry

    lax.fori_loop(0, slots, clear, 0, unroll=4)
    lax.fori_loop(0, slots // CAP, forget, 0, unroll=4)
    lax.fori_loop(0, step_count * tile_count, place, 0)
    lax.fori_loop(0, slots, fill, 0, unroll=2)


def pack_tiles(tiles, dest, owners):
    slots = owners * CAP
    rows, width = tiles.shape[1:]
    vmem = pl.BlockSpec(memory_space=pltpu.VMEM)
    return pl.pallas_call(
        pack_kernel,
        out_shape=jax.ShapeDtypeStruct((slots, rows // lax.axis_size("kgrp"), width), tiles.dtype),
        in_specs=[pl.BlockSpec(memory_space=pltpu.SMEM), vmem],
        out_specs=vmem,
        scratch_shapes=[pltpu.SMEM((owners,), jnp.int32), pltpu.SMEM((slots,), jnp.int32)],
        compiler_params=pltpu.CompilerParams(vmem_limit_bytes=MUCH),
        cost_estimate=pl.CostEstimate(flops=0, bytes_accessed=0, transcendentals=0),
        name="pack_tiles",
    )(dest, tiles)


def weight_kernel(slot_count, *refs):
    sources, (weight_ref, point_ref, cell_ref, dest_ref, column_ref, sems) = refs[:4], refs[4:]
    copies = [
        pltpu.make_async_copy(source, target, sems.at[index])
        for index, (source, target) in enumerate(zip(sources, (point_ref, cell_ref, dest_ref, column_ref)))
    ]
    for copy in copies:
        copy.start()
    for copy in copies:
        copy.wait()
    tile_count, _, vectors = dest_ref.shape
    owners = weight_ref.shape[1] // LANES
    step_count = vectors // owners
    k_count = point_ref.shape[0]
    mine = dest_ref[:, 0, :] == lax.axis_index("orb")
    flags = mine.astype(jnp.float32)
    shape = (tile_count, tile_count)
    before = lax.broadcasted_iota(jnp.int32, shape, 1) < lax.broadcasted_iota(jnp.int32, shape, 0)
    rank = jnp.dot(before.astype(jnp.float32), flags, preferred_element_type=jnp.float32)
    shape = (vectors, vectors)
    sooner, later = lax.broadcasted_iota(jnp.int32, shape, 0), lax.broadcasted_iota(jnp.int32, shape, 1)
    same_owner = (sooner < later) & (sooner >= later - later % step_count)
    counts = jnp.broadcast_to(jnp.sum(flags, axis=0, keepdims=True), (8, vectors))
    above = jnp.dot(counts, same_owner.astype(jnp.float32), preferred_element_type=jnp.float32)
    rank = (rank + above[0:1]).astype(jnp.int32)
    cells = cell_ref[...].astype(jnp.float32)
    column = column_ref[...]
    values = []
    for k in range(k_count):
        fraction = point_ref[k, 0] * cells[0:1] + point_ref[k, 1] * cells[1:2]
        fraction = fraction + point_ref[k, 2] * cells[2:3]
        radians = 6.283185307179586 * fraction
        for wave in (jnp.cos(radians), jnp.sin(radians)):
            phase = wave.astype(jnp.bfloat16).astype(jnp.float32)
            for j in range(slot_count):
                for c in range(CAP):
                    here = mine & (rank == c) & (column == j)
                    values.append(jnp.sum(jnp.where(here, phase, 0.0), axis=0, keepdims=True))
    values = jnp.concatenate(values, axis=0)
    chunk = math.gcd(owners, 16)
    shape = (vectors, chunk * LANES)
    for first in range(0, owners, chunk):
        owner = first + lax.broadcasted_iota(jnp.int32, shape, 1) // LANES
        member = (lax.broadcasted_iota(jnp.int32, shape, 0) // step_count == owner).astype(jnp.float32)
        weight_ref[:, first * LANES : (first + chunk) * LANES] = jnp.dot(
            values, member, preferred_element_type=jnp.float32
        )


def receive_weights(kpoints, cells, dest, column, owners, slot_count):
    k_count = kpoints.shape[0]
    operands = (kpoints, cells, dest, column)
    spaces = (pltpu.SMEM, pltpu.VMEM, pltpu.VMEM, pltpu.VMEM)
    return pl.pallas_call(
        functools.partial(weight_kernel, slot_count),
        out_shape=jax.ShapeDtypeStruct((k_count * 2 * slot_count * CAP, owners * LANES), jnp.float32),
        in_specs=[pl.BlockSpec(memory_space=pltpu.HBM)] * 4,
        out_specs=pl.BlockSpec(memory_space=pltpu.VMEM),
        scratch_shapes=[space(array.shape, array.dtype) for space, array in zip(spaces, operands)]
        + [pltpu.SemaphoreType.DMA((4,))],
        compiler_params=pltpu.CompilerParams(vmem_limit_bytes=LITTLE),
        cost_estimate=pl.CostEstimate(flops=0, bytes_accessed=0, transcendentals=0),
        name="receive_weights",
    )(*operands)


def add_tiles(weight_ref, tiles_ref, pair_ref, index, k_count, slot_count):
    slots, part, width = tiles_ref.shape
    rows = pair_ref.shape[1] // 2
    band = slot_count * width
    kinds = k_count * 2 * slot_count

    def add(owner, totals):
        lanes = pl.ds(pl.multiple_of(owner * LANES, LANES), LANES)
        for c in range(CAP):
            tile = tiles_ref[owner * CAP + c].astype(jnp.float32)
            totals = tuple(
                total + weight_ref[pl.ds(kind * CAP + c, 1), lanes] * tile for kind, total in enumerate(totals)
            )
        return totals

    totals = lax.fori_loop(
        0, slots // CAP, add, tuple(jnp.zeros((part, width), jnp.float32) for _ in range(kinds))
    )
    top = pl.ds(pl.multiple_of(index * part, part), part)
    bottom = pl.ds(pl.multiple_of(rows + index * part, part), part)
    for k in range(k_count):
        for p in range(2):
            for j in range(slot_count):
                value = totals[(k * 2 + p) * slot_count + j].astype(jnp.bfloat16)
                columns = slice(j * width, (j + 1) * width)
                later = slice(band + j * width, band + (j + 1) * width)
                if p == 0:
                    pair_ref[k, top, columns] = value
                    pair_ref[k, bottom, later] = value
                else:
                    pair_ref[k, bottom, columns] = value
                    pair_ref[k, top, later] = -value


def begin_kernel(k_count, slot_count, weight_ref, tiles_ref, pair_ref):
    add_tiles(weight_ref, tiles_ref, pair_ref, lax.axis_index("kgrp"), k_count, slot_count)


def band_kernel(k_count, slot_count, weight_ref, tiles_ref, begun_ref, pair_ref, core_ref, chip_ref):
    rows = pair_ref.shape[1] // 2
    band = core_ref.shape[-1]
    pair_ref[...] = begun_ref[...]
    add_tiles(weight_ref, tiles_ref, pair_ref, 1 - lax.axis_index("kgrp"), k_count, slot_count)
    odd_core = lax.axis_index("orb") & 1
    for odd in (0, 1):

        @pl.when(odd_core == odd)
        def _():
            tail_ref, head_ref = (chip_ref, core_ref) if odd else (core_ref, chip_ref)
            for k in range(k_count):
                for p in range(2):
                    tail_ref[k, p] = pair_ref[k, (p + 1) * rows - HALO : (p + 1) * rows, 0:band]
                    head_ref[k, p] = pair_ref[k, p * rows : p * rows + HALO, 0:band]


def begin_bands(weights, tiles, k_count, slot_count):
    part, width = tiles.shape[1:]
    vmem = pl.BlockSpec(memory_space=pltpu.VMEM)
    return pl.pallas_call(
        functools.partial(begin_kernel, k_count, slot_count),
        out_shape=jax.ShapeDtypeStruct((k_count, 4 * part, 2 * slot_count * width), jnp.bfloat16),
        in_specs=[vmem, vmem],
        out_specs=vmem,
        compiler_params=pltpu.CompilerParams(vmem_limit_bytes=LITTLE),
        cost_estimate=pl.CostEstimate(flops=0, bytes_accessed=0, transcendentals=0),
        name="begin_bands",
    )(weights, tiles)


def make_bands(weights, tiles, begun, k_count, slot_count):
    band = slot_count * tiles.shape[2]
    edge = (k_count, 2, HALO, band)
    vmem = pl.BlockSpec(memory_space=pltpu.VMEM)
    return pl.pallas_call(
        functools.partial(band_kernel, k_count, slot_count),
        out_shape=[jax.ShapeDtypeStruct(shape, jnp.bfloat16) for shape in (begun.shape, edge, edge)],
        in_specs=[vmem, vmem, vmem],
        out_specs=[vmem, vmem, vmem],
        compiler_params=pltpu.CompilerParams(vmem_limit_bytes=LITTLE),
        cost_estimate=pl.CostEstimate(flops=0, bytes_accessed=0, transcendentals=0),
        name="make_bands",
    )(weights, tiles, begun)


def filter_kernel(places, pair_source, core_ref, chip_ref, own_ref, sibling_ref, *rest):
    pieces = len(places)
    chip_refs, onward_refs, near_chip_refs, near_onward_refs = (
        rest[part * pieces : (part + 1) * pieces] for part in range(4)
    )
    result_ref, pair_ref, window, done, edges, band_sems, sems, done_sems = rest[-8:]
    chunks, _, block = window.shape
    k_count, double_rows, _ = pair_ref.shape
    rows = double_rows // 2
    band = core_ref.shape[-1]
    per_piece = chunks // pieces
    group = lax.axis_index("kgrp")
    state = lax.axis_index("orb") & 3
    starts = [0, HALO, HALO + rows, HALO + 2 * rows, HALO + 3 * rows]

    def columns_of(chunk):
        fixed, by_group, _ = places[chunk // per_piece]
        first = fixed + by_group * group + chunk % per_piece * block
        return pl.ds(pl.multiple_of(first, block), block)

    bands = [
        pltpu.make_async_copy(pair_source, pair_ref, band_sems.at[0]),
        pltpu.make_async_copy(core_ref, edges.at[1 - (state & 1)], band_sems.at[1]),
        pltpu.make_async_copy(chip_ref, edges.at[state & 1], band_sems.at[2]),
    ]
    for copy in bands:
        copy.start()
    for odd_chip in (0, 1):
        for odd_core in (0, 1):

            @pl.when(state == odd_chip * 2 + odd_core)
            def _():
                for chunk in range(chunks):
                    whole = columns_of(chunk)
                    index, place = chunk // per_piece, chunk % per_piece
                    piece = pl.ds(place * block, block)
                    sibling = sibling_ref.at[:, whole]
                    low = places[index][2]
                    near = near_chip_refs[index].at[0:rows, piece]
                    if odd_chip == odd_core:
                        near = near_onward_refs[index].at[0:rows, piece]
                    before, beyond = (chip_refs[index], 0), (onward_refs[index], low)
                    if odd_chip == 0:
                        before, beyond = beyond, before
                    (before, last), (beyond, first) = before, beyond
                    sources = [
                        before.at[last + rows - HALO : last + rows, piece],
                        sibling if odd_core else near,
                        own_ref.at[:, whole],
                        near if odd_core else sibling,
                        beyond.at[first : first + HALO, piece],
                    ]
                    for part, source in enumerate(sources):
                        count = source.shape[0]
                        target = window.at[chunk, starts[part] : starts[part] + count, :]
                        pltpu.make_async_copy(source, target, sems.at[chunk, part]).start()

    for copy in bands:
        copy.wait()

    def product(left, right):
        return jnp.dot(left, right, preferred_element_type=jnp.float32)

    own_band = jnp.concatenate([pair_ref[k][:, 0:band] for k in range(k_count)], axis=0)
    halo_rows = k_count * 2 * HALO

    def result_copy(chunk):
        return pltpu.make_async_copy(
            done.at[chunk], result_ref.at[:, :, :, columns_of(chunk)], done_sems.at[chunk]
        )

    for chunk in range(chunks):
        for part in range(5):
            count = HALO if part in (0, 4) else rows
            target = window.at[chunk, starts[part] : starts[part] + count, :]
            pltpu.make_async_copy(target, target, sems.at[chunk, part]).wait()
        lower = window[chunk, 0:band, :]
        middle = window[chunk, rows : rows + band, :]
        upper = window[chunk, 2 * rows : 2 * rows + band, :]
        own_first = product(own_band, middle).astype(jnp.bfloat16)
        left_first = product(edges[0].reshape(halo_rows, band), lower).astype(jnp.bfloat16)
        right_first = product(edges[1].reshape(halo_rows, band), upper).astype(jnp.bfloat16)
        center = window[chunk, HALO + rows : HALO + 2 * rows, :].astype(jnp.float32)
        for k in range(k_count):
            wide = jnp.concatenate(
                [
                    part
                    for kind in (2 * k, 2 * k + 1)
                    for part in (
                        left_first[kind * HALO : (kind + 1) * HALO],
                        own_first[kind * rows : (kind + 1) * rows],
                        right_first[kind * HALO : (kind + 1) * HALO],
                    )
                ],
                axis=0,
            )
            both = 2.0 * product(pair_ref[k], wide)
            done[chunk, k, 0] = (both[0:rows] - center).astype(jnp.bfloat16)
            done[chunk, k, 1] = both[rows:].astype(jnp.bfloat16)
        result_copy(chunk).start()
    for chunk in range(chunks):
        result_copy(chunk).wait()


def filter_columns(places, pair, core_band, chip_band, own, sibling, halos, so_far):
    k_count, double_rows, _ = pair.shape
    rows = double_rows // 2
    columns = own.shape[1]
    pieces = len(halos)
    width = halos[0][0].shape[1]
    block = min(BLOCK, width)
    chunks = pieces * width // block
    anywhere = pl.BlockSpec(memory_space=pl.ANY)
    hbm = pl.BlockSpec(memory_space=pltpu.HBM)
    operands = [pair, core_band, chip_band, own, sibling]
    operands += [halo[part] for part in range(4) for halo in halos]
    specs = [anywhere] * (5 + 4 * pieces)
    aliases = {}
    if so_far is not None:
        aliases = {len(operands): 0}
        operands.append(so_far)
        specs.append(hbm)
    return pl.pallas_call(
        functools.partial(filter_kernel, places),
        out_shape=jax.ShapeDtypeStruct((k_count, 2, rows, columns), jnp.bfloat16),
        in_specs=specs,
        out_specs=hbm,
        scratch_shapes=[
            pltpu.VMEM(pair.shape, jnp.bfloat16),
            pltpu.VMEM((chunks, 3 * rows + 2 * HALO, block), jnp.bfloat16),
            pltpu.VMEM((chunks, k_count, 2, rows, block), jnp.bfloat16),
            pltpu.VMEM((2,) + core_band.shape, jnp.bfloat16),
            pltpu.SemaphoreType.DMA((3,)),
            pltpu.SemaphoreType.DMA((chunks, 5)),
            pltpu.SemaphoreType.DMA((chunks,)),
        ],
        input_output_aliases=aliases,
        compiler_params=pltpu.CompilerParams(vmem_limit_bytes=49 << 20),
        cost_estimate=pl.CostEstimate(
            flops=0,
            bytes_accessed=0,
            transcendentals=0,
        ),
        name="filter_columns",
    )(*operands)


def local(hopping_tiles, tile_strip, tile_column_slot, lattice, kpoints, start_block):
    owners = lax.axis_size("orb")
    group = lax.axis_index("kgrp")
    step_count, tile_count, row_count, col_width = hopping_tiles.shape
    slot_count = (row_count + 2 * HALO) // col_width
    k_count = kpoints.shape[0]
    piece = start_block.shape[1] // 4

    dest = jnp.transpose(tile_strip, (1, 2, 0))
    tiles = hopping_tiles.reshape(step_count * tile_count, row_count, col_width)
    outgoing = pack_tiles(tiles, dest, owners)
    weights = receive_weights(kpoints, lattice.T, dest, tile_column_slot.T, owners, slot_count)
    incoming = lax.all_to_all(outgoing, "orb", split_axis=0, concat_axis=0, tiled=True)

    shared = to_pair_chip(lax.dynamic_slice_in_dim(start_block, group * piece, piece, axis=1))
    shared = after(shared, outgoing)
    third = to_pair_chip(after(start_block, shared)[:, 2 * piece : 3 * piece])
    near_shared = to_sibling(shared)
    sibling = to_sibling(start_block)
    shared_beyond = onward(shared)

    last = after(start_block, shared)[:, 3 * piece : 4 * piece]
    begun = begin_bands(weights, after(incoming, near_shared, sibling, last), k_count, slot_count)
    theirs = to_other_group(after(incoming, begun))
    third = after(third, begun)
    fourth = to_pair_chip(after(last, third, shared_beyond))
    third_beyond = onward(third)
    pair, for_core, for_chip = make_bands(weights, theirs, begun, k_count, slot_count)
    core_band, chip_band = to_sibling(for_core), to_next_chip(for_chip)

    other = to_other_group(after(jnp.concatenate([shared, shared_beyond], axis=0), pair))
    fourth = after(fourth, core_band, chip_band)
    third_beyond = after(third_beyond, fourth)
    near_shared_beyond = to_sibling(after(shared_beyond, chip_band))
    near_third_beyond = to_sibling(third_beyond)
    near_third = to_sibling(after(third, pair))
    fourth_beyond = onward(fourth)
    near_fourth = to_sibling(fourth)

    def filtered(places, halos, so_far):
        return filter_columns(places, pair, core_band, chip_band, start_block, sibling, halos, so_far)

    result = filtered(
        [(0, piece, 0), (2 * piece, 0, 0)],
        [
            (shared, shared_beyond, near_shared, near_shared_beyond),
            (third, third_beyond, near_third, near_third_beyond),
        ],
        None,
    )
    other, fourth_beyond = after(other, result), after(fourth_beyond, result)
    owner = lax.axis_index("orb")
    near_other = to_sibling(jnp.where((owner >> 1) & 1 == owner & 1, other[:row_count], other[row_count:]))
    return filtered(
        [(piece, -piece, row_count), (3 * piece, 0, 0)],
        [
            (other, other, near_other, near_other),
            (fourth, fourth_beyond, near_fourth, to_sibling(fourth_beyond)),
        ],
        result,
    )


def solution(mesh):
    return jax.shard_map(
        local,
        mesh=mesh,
        in_specs=(P("orb", None, None, None), P(), P(), P(), P("kgrp", None), P("orb", None)),
        out_specs=P("kgrp", None, "orb", None),
        check_vma=False,
    )
```
